32 devices in a mesh: tm: 8 (over z, x), chan: 4 (over y, core).
Axes of the slice: x: 2, y: 2, z: 4, core: 2. Of those that a mesh axis runs over, the one named last changes fastest.
Arguments:
- inner_x: bfloat16 [512, 1152], P('tm', 'chan'), may hold values from -6 to 6
- gate_z: bfloat16 [512, 1152], P('tm', 'chan'), may hold values from -6 to 6
- dt_raw: bfloat16 [512, 1152], P('tm', 'chan'), may hold values from -3 to 3
- grad_out: bfloat16 [512, 1152], P('tm', 'chan'), may hold values from -6 to 6
- input_b: bfloat16 [512, 16], P('tm'), may hold values from -1.5 to 1.5
- output_c: bfloat16 [512, 16], P('tm'), may hold values from -1.5 to 1.5
- conv_weight: float32 [4, 1152], P(None, 'chan'), may hold values from -3 to 3
- conv_bias: float32 [1152], P('chan'), may hold values from -0.5 to 0.5
- decay_log: float32 [16, 1152], P(None, 'chan'), as said below
- skip_gain: float32 [1152], P('chan'), may hold values from 0.5 to 1.5
Outputs:
- grad_x: bfloat16 [512, 1152], P('tm', 'chan')
- grad_dt: bfloat16 [512, 1152], P('tm', 'chan')
- grad_z: bfloat16 [512, 1152], P('tm', 'chan')
- grad_b: bfloat16 [512, 16], P('tm')
- grad_c: bfloat16 [512, 16], P('tm')
The draws below stay inside these ranges and needn't reach their ends.
Inputs may be any that keep to these rules, and one draw needn't show every extreme that they name: `decay_log`: each entry is the natural logarithm of a positive decay rate.
All inputs are finite; a program needn't handle non-finite values.
Results may differ from the reference program's by a relative error of at most 0.0085.
Values may be sent and summed in bfloat16 or wider, within the bound.
A program may use at most 64 MiB of HBM per device.

```python
import math
import jax
import jax.numpy as jnp
from jax import lax

E = 1152
N = 16
CONV = 4
FRAMES = 32
SPATIAL = 16
TOKENS = 512


def draw_decay_log(key, part):
    lower = math.log(0.05 / TOKENS)
    upper = math.log(0.06)
    return jax.random.uniform(jax.random.fold_in(key, 10), (N, E), jnp.float32, lower, upper)


def level_of(rng, extent, cuts, low, high):
    def one(dim, parts):
        draws = jax.random.uniform(jax.random.fold_in(jax.random.fold_in(rng, 6), dim), (parts,), jnp.float32, low / len(cuts), high / len(cuts))
        return jnp.repeat(jnp.exp(draws), extent[dim] // parts).reshape((-1,) + (1,) * (len(extent) - dim - 1))

    loudness = one(*cuts[0])
    for cut in cuts[1:]:
        loudness = loudness * one(*cut)
    return loudness


def centred(stream_key, extent, spread, most, pieces=(), kind=jnp.bfloat16):
    factor_of = level_of(stream_key, extent, pieces, -0.22, 0.18) if pieces else 1.0
    values = jax.random.normal(stream_key, extent, jnp.float32) * spread * factor_of
    return jnp.minimum(jnp.maximum(values, -most), most).astype(kind)


def setup_inputs(seed: int = 0) -> dict:
    keys = jax.random.split(jax.random.key(seed), 11)
    return {
        "inner_x": centred(keys[0], (TOKENS, E), 1.0, 6.0, ((0, 8), (1, 4))),
        "gate_z": centred(keys[1], (TOKENS, E), 1.0, 6.0, ((0, 8), (1, 4))),
        "dt_raw": centred(keys[2], (TOKENS, E), 0.5, 3.0, ((0, 8), (1, 4))),
        "grad_out": centred(keys[3], (TOKENS, E), 1.0, 6.0, ((0, 8), (1, 4))),
        "input_b": centred(keys[4], (TOKENS, N), (0.5 / (TOKENS ** 0.25)), 1.5, ((0, 8),)),
        "output_c": centred(keys[5], (TOKENS, N), (0.5 / (TOKENS ** 0.25)), 1.5, ((0, 8),)),
        "conv_weight": centred(keys[6], (CONV, E), CONV ** -0.5, 3.0, ((1, 4),), jnp.float32),
        "conv_bias": jnp.clip(jax.random.uniform(keys[7], (E,), jnp.float32, -0.5, 0.5) * level_of(keys[7], (E,), ((0, 4),), -0.4, 0.0), -0.5, 0.5),
        "decay_log": draw_decay_log(jax.random.fold_in(keys[10], 71), 0),
        "skip_gain": jnp.clip(0.5 + 1.0 * jax.random.uniform(keys[9], (E,), jnp.float32) ** level_of(keys[9], (E,), ((0, 4),), -0.2, 0.2), 0.5, 1.5),
    }


def silu_grad(values):
    sigm = jax.nn.sigmoid(values)
    return sigm * (1.0 + values * (1.0 - sigm))

def to_sequence(array):
    return jnp.swapaxes(array.reshape(FRAMES, SPATIAL, array.shape[-1]), 0, 1).reshape(TOKENS, array.shape[-1])

def from_sequence(array):
    return jnp.swapaxes(array.reshape(SPATIAL, FRAMES, array.shape[-1]), 0, 1).reshape(TOKENS, array.shape[-1])

def scan_forward(inner, dt_values, in_b, out_c, conv_weight, conv_bias, decay_rate, skip_gain):
    deltas = jax.nn.softplus(dt_values)
    padded = jnp.concatenate([jnp.zeros((CONV - 1, E), jnp.float32), inner])
    pre_act = conv_bias[None, :] + jnp.zeros((TOKENS, E), jnp.float32)
    for offset in range(CONV):
        pre_act = pre_act + conv_weight[offset][None, :] * padded[offset:offset + TOKENS]
    conv_out = jax.nn.silu(pre_act)
    block_len = math.gcd(TOKENS, 256)
    count = TOKENS // block_len

    def token_step(state, items):
        delta_row, conv_row, b_row, c_row = items
        state = jnp.exp(delta_row[None, :] * decay_rate) * state + (delta_row * conv_row)[None, :] * b_row[:, None]
        return (state, lax.optimization_barrier(jnp.sum(c_row[:, None] * state, axis=0)))

    def block_body(state, items):
        return lax.scan(token_step, state, items)
    block_step = jax.checkpoint(block_body)
    items = (deltas.reshape(count, block_len, E), conv_out.reshape(count, block_len, E), in_b.reshape(count, block_len, N), out_c.reshape(count, block_len, N))
    init_state = jnp.zeros((N, E), jnp.float32)
    outputs = lax.scan(block_step, init_state, items)[1]
    return outputs.reshape(TOKENS, E) + skip_gain[None, :] * conv_out

def reference(inner_x, gate_z, dt_raw, grad_out, input_b, output_c, conv_weight, conv_bias, decay_log, skip_gain):
    seq_x = to_sequence(inner_x).astype(jnp.float32)
    seq_z = to_sequence(gate_z).astype(jnp.float32)
    seq_dt = to_sequence(dt_raw).astype(jnp.float32)
    seq_grad = to_sequence(grad_out).astype(jnp.float32)
    seq_b = to_sequence(input_b).astype(jnp.float32)
    seq_c = to_sequence(output_c).astype(jnp.float32)
    decay_rate = -jnp.exp(decay_log)

    def mapped(inner, dt_values, in_b, out_c):
        return scan_forward(inner, dt_values, in_b, out_c, conv_weight, conv_bias, decay_rate, skip_gain)
    seq_full, pullback = jax.vjp(mapped, seq_x, seq_dt, seq_b, seq_c)
    seq_y = seq_full.astype(jnp.bfloat16)
    seq_dy = (seq_grad * jax.nn.silu(seq_z)).astype(jnp.bfloat16)
    grad_sx, grad_sdt, grad_sb, grad_sc = pullback(seq_dy.astype(jnp.float32))
    grad_sz = seq_grad * seq_y.astype(jnp.float32) * silu_grad(seq_z)
    return (from_sequence(grad_sx).astype(jnp.bfloat16), from_sequence(grad_sdt).astype(jnp.bfloat16), from_sequence(grad_sz).astype(jnp.bfloat16), from_sequence(grad_sb).astype(jnp.bfloat16), from_sequence(grad_sc).astype(jnp.bfloat16))
```

```python
import functools

import jax
import jax.numpy as jnp
from jax import lax
from jax.experimental import pallas as pl
from jax.experimental.pallas import tpu as pltpu
from jax.sharding import PartitionSpec as P

S_DEV = 2
BLK = 16
F32 = jnp.float32
BF16 = jnp.bfloat16
MESH = pl.DeviceIdType.MESH


def log2(value):
    assert value & (value - 1) == 0
    return value.bit_length() - 1


def dot(left, right):
    return jnp.dot(left, right, preferred_element_type=F32)


def iotas(shape):
    return lax.broadcasted_iota(jnp.int32, shape, 0), lax.broadcasted_iota(jnp.int32, shape, 1)


def ones_where(mask):
    return jnp.where(mask, 1.0, 0.0).astype(BF16)


def fields(packed, half, per, frames):
    partner = packed >> log2(2 * per)
    inside = packed & (2 * per - 1)
    rest = inside & (per - 1)
    spatial = rest >> log2(frames)
    frame = rest & (frames - 1)
    valid = (inside >> log2(per)) == half
    return partner, spatial, frame, valid


def row_of(packed, half, tm, per, frames):
    partner, spatial, frame, valid = fields(packed, half, per, frames)
    row = frame * (S_DEV * tm) + partner * S_DEV + spatial
    return jnp.where(valid, row, -1)


def place_of(packed, half, tm, per, frames):
    partner, spatial, frame, valid = fields(packed, half, per, frames)
    place = spatial * (frames * tm) + partner * frames + frame
    return jnp.where(valid, place, -1)


def pack_matrix(of, half, tm, per, frames, length):
    packed, row = iotas((tm * 2 * per, length))
    return ones_where(of(packed, half, tm, per, frames) == row)


def unpack_matrix(of, half, tm, per, frames, length):
    row, packed = iotas((length, tm * 2 * per))
    return ones_where(of(packed, half, tm, per, frames) == row)


def sigmoid(values):
    return 1.0 / (1.0 + jnp.exp(-values))


def silu_grad(values):
    sigm = sigmoid(values)
    return sigm * (1.0 + values * (1.0 - sigm))


def kernel(
    tm,
    chan,
    x_ref,
    z_ref,
    dt_ref,
    g_ref,
    b_ref,
    c_ref,
    w_ref,
    bias_ref,
    log_ref,
    skip_ref,
    out_a,
    out_b,
    send_1,
    send_2,
    send_h,
    recv_1,
    recv_2,
    recv_h,
    ends,
    ends_in,
    part,
    part_in,
    edge,
    edge_in,
    send_a,
    send_b,
    xpad,
    pre_s,
    conv_s,
    delta_s,
    u_s,
    dy_s,
    dt_s,
    z_s,
    g_s,
    y_s,
    w_s,
    d_s,
    gp_s,
    bc_s,
    fs_s,
    prod,
    sem_1,
    sem_2,
    sem_h,
    sem_e,
    sem_p,
    sem_g,
    sem_a,
    sem_b,
):
    me = lax.axis_index("tm")
    ch = lax.axis_index("chan")
    length, width = x_ref.shape
    states = b_ref.shape[1]
    taps = w_ref.shape[0]
    frames = length // (S_DEV * tm)
    per = S_DEV * frames
    wide = width + 2 * states
    base = width // 128 * 128

    def partner(k):
        return lax.rem(me + k, tm)

    def peer(k):
        return lax.rem(ch + k, chan)

    def over_tm(body):
        def step(k, carry):
            body(partner(k))
            return carry

        lax.fori_loop(1, tm, step, 0)

    def over_chan(body):
        for k in range(1, chan):
            body(peer(k))

    barrier = pltpu.get_barrier_semaphore()

    def greet(d):
        pl.semaphore_signal(barrier, inc=1, device_id={"tm": d}, device_id_type=MESH)

    def greet_peer(d):
        pl.semaphore_signal(barrier, inc=1, device_id={"chan": d}, device_id_type=MESH)

    over_tm(greet)
    over_chan(greet_peer)

    row, lane = iotas((width, wide))
    ex = ones_where(row == lane)
    row, lane = iotas((states, wide))
    eb = ones_where(lane == row + width)
    ec = ones_where(lane == row + width + states)
    x_ext = (dot(x_ref[...], ex) + dot(b_ref[...], eb) + dot(c_ref[...], ec)).astype(BF16)
    first = pack_matrix(row_of, 0, tm, per, frames, length)
    second = pack_matrix(row_of, 1, tm, per, frames, length)
    dt_ext = dot(dt_ref[...], ex).astype(BF16)
    one = (dot(first, x_ext) + dot(second, dt_ext)).astype(BF16)
    two = (dot(first, z_ref[...]) + dot(second, g_ref[...])).astype(BF16)
    send_1[...] = one.reshape(tm, 2 * per, wide)
    send_2[...] = two.reshape(tm, 2 * per, width)
    packed, row = iotas((tm * 16, length))
    slot = packed & 15
    frame = slot - (8 - frames)
    source = frame * (S_DEV * tm) + (packed >> 4) * S_DEV - 1
    good = (frame >= 0) & (slot < 8) & (packed >= 16)
    halo = ones_where(jnp.where(good, source, -1) == row)
    send_h[...] = dot(halo, x_ref[...]).astype(BF16).reshape(tm, 16, width)

    pl.semaphore_wait(barrier, tm - 1 + chan - 1)

    def copy_tm(src, dst, sems, d, origin):
        return pltpu.make_async_remote_copy(
            src_ref=src,
            dst_ref=dst,
            send_sem=sems.at[0, d],
            recv_sem=sems.at[1, origin],
            device_id={"tm": d},
            device_id_type=MESH,
        )

    def copy_1(d, origin):
        return copy_tm(send_1.at[d], recv_1.at[origin], sem_1, d, origin)

    def copy_2(d, origin):
        return copy_tm(send_2.at[d], recv_2.at[origin], sem_2, d, origin)

    def copy_h(d):
        return pltpu.make_async_remote_copy(
            src_ref=send_h.at[d],
            dst_ref=recv_h,
            send_sem=sem_h.at[d],
            recv_sem=sem_h.at[tm],
            device_id={"tm": d},
            device_id_type=MESH,
        )

    def start_halo(d):
        @pl.when(me == tm - 1)
        def _():
            copy_h(d).start()

    over_tm(start_halo)
    over_tm(lambda d: copy_1(d, me).start())
    over_tm(lambda d: copy_2(d, me).start())
    recv_1[me] = send_1[me]
    recv_2[me] = send_2[me]

    rate = -jnp.exp(log_ref[...])
    take_0 = unpack_matrix(place_of, 0, tm, per, frames, length)
    take_1 = unpack_matrix(place_of, 1, tm, per, frames, length)
    row, lane = iotas((BLK, BLK * states))
    sel = ones_where((lane >> log2(states)) == row)
    row, lane = iotas((BLK * states, BLK))
    spread = ones_where((row >> log2(states)) == lane)

    @pl.when(me == tm - 1)
    def _():
        recv_h[...] = send_h[me]

    @pl.when(me != tm - 1)
    def _():
        copy_h(me).wait_recv()

    over_tm(lambda d: copy_1(d, d).wait_recv())
    got_1 = recv_1[...].reshape(tm * 2 * per, wide)
    x_full = dot(take_0, got_1)
    dt_vals = dot(take_1, got_1[:, :width])
    xpad[0:8, :] = recv_h[...].astype(F32)[0:8]
    xpad[8:, :] = x_full[:, :width]
    tail = wide - base
    bc_bf = x_full[:, base:].astype(BF16)
    row, lane = iotas((BLK * states, tail))
    keep = ((lane - (width - base)) & (states - 1)) == (row & (states - 1))
    keep = keep & (lane >= width - base)
    row, lane = iotas((tail, 256))
    fan = ones_where(
        (row >= width - base)
        & (((row - (width - base)) >> log2(states)) == (lane >> 7))
    )
    for block in range(length // BLK):
        rows = dot(spread, bc_bf[block * BLK : (block + 1) * BLK])
        rows = jnp.where(keep, rows, 0.0).astype(BF16)
        bc_s[block * BLK * states : (block + 1) * BLK * states, :] = dot(rows, fan)

    dt_s[...] = dt_vals
    deltas = jnp.maximum(dt_vals, 0.0) + jnp.log(1.0 + jnp.exp(-jnp.abs(dt_vals)))
    delta_s[...] = deltas
    pre = bias_ref[...] + w_ref[0:1, :] * xpad[8 - taps + 1 : 8 - taps + 1 + length, :]
    for k in range(1, taps):
        pre = pre + w_ref[k : k + 1, :] * xpad[8 - taps + 1 + k : 8 - taps + 1 + k + length, :]
    pre_s[...] = pre
    conv = pre * sigmoid(pre)
    conv_s[...] = conv
    u_s[...] = deltas * conv
    total = jnp.sum(deltas, axis=0, keepdims=True)

    over_tm(lambda d: copy_2(d, d).wait_recv())
    got_2 = recv_2[...].reshape(tm * 2 * per, width)
    z_vals = dot(take_0, got_2)
    g_vals = dot(take_1, got_2)
    z_s[...] = z_vals
    g_s[...] = g_vals
    dy_s[...] = (g_vals * (z_vals * sigmoid(z_vals))).astype(BF16).astype(F32)

    def over_lanes(tile):
        return jnp.concatenate([tile] * (width // 128) + [tile[:, : width % 128]], axis=1)

    def b_at(q):
        return over_lanes(bc_s[pl.ds(pl.multiple_of(q * states, states), states), 0:128])

    def c_at(q):
        return over_lanes(bc_s[pl.ds(pl.multiple_of(q * states, states), states), 128:256])

    zero = jnp.zeros((states, width), F32)

    def local(i, carry):
        state, back = carry
        up = pl.multiple_of(i * 8, 8)
        down = pl.multiple_of(length - 8 - i * 8, 8)
        d_up, u_up = delta_s[pl.ds(up, 8), :], u_s[pl.ds(up, 8), :]
        d_dn, y_dn = delta_s[pl.ds(down, 8), :], dy_s[pl.ds(down, 8), :]
        for j in range(8):
            state = jnp.exp(d_up[j : j + 1] * rate) * state + u_up[j : j + 1] * b_at(up + j)
            m = 7 - j
            back = jnp.exp(d_dn[m : m + 1] * rate) * (y_dn[m : m + 1] * c_at(down + m) + back)
        return state, back

    end, back_end = lax.fori_loop(0, length // 8, local, (zero, zero))
    row = lax.broadcasted_iota(jnp.int32, (16, width), 0)
    high = total.astype(BF16).astype(F32)
    sums = jnp.where(row == 0, high, jnp.where(row == 1, total - high, 0.0))
    ends[0:16, :] = end.astype(BF16)
    ends[16:32, :] = sums.astype(BF16)
    ends[32:48, :] = back_end.astype(BF16)

    def copy_up(d, origin):
        return copy_tm(ends.at[0:32], ends_in.at[origin, 0:32], sem_e, d, origin)

    def copy_down(d, origin):
        return copy_tm(ends.at[16:48], ends_in.at[origin, 16:48], sem_e, d, origin)

    def send_end(d):
        @pl.when(d > me)
        def _():
            copy_up(d, me).start()

        @pl.when(d < me)
        def _():
            copy_down(d, me).start()

    over_tm(send_end)

    def through(source):
        pair = ends_in[source, 16:32, :].astype(F32)
        return jnp.exp(rate * (pair[0:1] + pair[1:2]))

    def enter_up(source, state):
        copy_up(source, source).wait_recv()
        return through(source) * state + ends_in[source, 0:16, :].astype(F32)

    def enter_down(turn, back):
        source = tm - 1 - turn
        copy_down(source, source).wait_recv()
        return through(source) * back + ends_in[source, 32:48, :].astype(F32)

    state_in = lax.fori_loop(0, me, enter_up, zero)
    back_in = lax.fori_loop(0, tm - 1 - me, enter_down, zero)

    row, lane = iotas((BLK * states, 128))
    at_b = lane == (row & (states - 1))
    at_c = lane == (row & (states - 1)) + states
    ones = jnp.ones((width, 128), BF16)
    skip = skip_ref[...]

    def picked(product, where):
        sums = jnp.where(where, dot(product, ones), 0.0)
        high = sums.astype(BF16)
        low = (sums - high.astype(F32)).astype(BF16)
        return dot(sel, high) + dot(sel, low)

    def forward(i, state):
        start = pl.multiple_of(i * BLK, BLK)
        here = pl.ds(start, BLK)
        d_blk, u_blk, y_blk = delta_s[here, :], u_s[here, :], dy_s[here, :]
        for j in range(BLK):
            kept = jnp.exp(d_blk[j : j + 1] * rate) * state
            state = kept + u_blk[j : j + 1] * b_at(start + j)
            fs_s[pl.ds(pl.multiple_of((start + j) * states, states), states), :] = kept
            prod[0, j * states : (j + 1) * states, :] = (c_at(start + j) * state).astype(BF16)
            prod[1, j * states : (j + 1) * states, :] = (y_blk[j : j + 1] * state).astype(BF16)
        y_s[here, :] = dot(sel, prod[0]) + skip * conv_s[here, :]
        part[here, :] = picked(prod[1], at_c)
        return state

    lax.fori_loop(0, length // BLK, forward, state_in)

    def backward(turn, back):
        start = pl.multiple_of(length - BLK - turn * BLK, BLK)
        here = pl.ds(start, BLK)
        d_blk, u_blk, y_blk = delta_s[here, :], u_s[here, :], dy_s[here, :]
        for j in reversed(range(BLK)):
            adjoint = y_blk[j : j + 1] * c_at(start + j) + back
            back = jnp.exp(d_blk[j : j + 1] * rate) * adjoint
            kept = fs_s[pl.ds(pl.multiple_of((start + j) * states, states), states), :]
            rows = slice(j * states, (j + 1) * states)
            prod[0, rows, :] = (adjoint * b_at(start + j)).astype(BF16)
            prod[1, rows, :] = (adjoint * u_blk[j : j + 1]).astype(BF16)
            prod[2, rows, :] = (adjoint * rate * kept).astype(BF16)
        w_s[here, :] = dot(sel, prod[0])
        d_s[here, :] = dot(sel, prod[2])
        part[here, :] = part[here, :] + picked(prod[1], at_b)
        return back

    lax.fori_loop(0, length // BLK, backward, back_in)

    def copy_part(d, origin):
        return pltpu.make_async_remote_copy(
            src_ref=part,
            dst_ref=part_in.at[origin],
            send_sem=sem_p.at[0, d],
            recv_sem=sem_p.at[1, origin],
            device_id={"chan": d},
            device_id_type=MESH,
        )

    over_chan(lambda d: copy_part(d, ch).start())
    deltas = delta_s[...]
    weighted = w_s[...]
    grad_pre = (skip * dy_s[...] + deltas * weighted) * silu_grad(pre_s[...])
    gp_s[0:length, :] = grad_pre
    edge[...] = grad_pre[0:8]

    def copy_edge(d):
        return pltpu.make_async_remote_copy(
            src_ref=edge,
            dst_ref=edge_in,
            send_sem=sem_g.at[0],
            recv_sem=sem_g.at[1],
            device_id={"tm": d},
            device_id_type=MESH,
        )

    before = jnp.maximum(me - 1, 0)

    @pl.when(me > 0)
    def _():
        copy_edge(before).start()

    give_0 = pack_matrix(place_of, 0, tm, per, frames, length)
    give_1 = pack_matrix(place_of, 1, tm, per, frames, length)
    grad_dt = ((d_s[...] + conv_s[...] * weighted) * sigmoid(dt_s[...])).astype(BF16)
    seq_y = y_s[...].astype(BF16).astype(F32)
    grad_z = (g_s[...] * seq_y * silu_grad(z_s[...])).astype(BF16)
    both = (dot(give_0, grad_dt) + dot(give_1, grad_z)).astype(BF16)
    send_a[...] = both.reshape(tm, 2 * per, width)

    def copy_a(d, origin):
        return copy_tm(send_a.at[d], out_a.at[origin], sem_a, d, origin)

    def copy_b(d, origin):
        return copy_tm(send_b.at[d], out_b.at[origin], sem_b, d, origin)

    over_tm(lambda d: copy_a(d, me).start())
    out_a[me] = send_a[me]

    @pl.when(me < tm - 1)
    def _():
        copy_edge(before).wait_recv()
        gp_s[length:, :] = edge_in[...]

    @pl.when(me == tm - 1)
    def _():
        gp_s[length:, :] = jnp.zeros((8, width), F32)

    grad_x = w_ref[0:1, :] * gp_s[taps - 1 : taps - 1 + length, :]
    for k in range(1, taps):
        grad_x = grad_x + w_ref[k : k + 1, :] * gp_s[taps - 1 - k : taps - 1 - k + length, :]
    x_part = dot(give_0, grad_x.astype(BF16))
    over_chan(lambda d: copy_part(d, d).wait_recv())
    part_in[ch] = part[...]
    bc = part_in[0]
    for k in range(1, chan):
        bc = bc + part_in[k]
    bc = jnp.concatenate([bc.astype(BF16), jnp.zeros((length, width - 128), BF16)], axis=1)
    send_b[...] = (x_part + dot(give_1, bc)).astype(BF16).reshape(tm, 2 * per, width)
    over_tm(lambda d: copy_b(d, me).start())
    out_b[me] = send_b[me]

    over_tm(lambda d: copy_1(d, me).wait_send())
    over_tm(lambda d: copy_2(d, me).wait_send())

    def end_halo(d):
        @pl.when(me == tm - 1)
        def _():
            copy_h(d).wait_send()

    over_tm(end_halo)

    def end_ends(d):
        @pl.when(d > me)
        def _():
            copy_up(d, me).wait_send()

        @pl.when(d < me)
        def _():
            copy_down(d, me).wait_send()

    over_tm(end_ends)
    over_chan(lambda d: copy_part(d, ch).wait_send())

    @pl.when(me > 0)
    def _():
        copy_edge(before).wait_send()

    over_tm(lambda d: copy_a(d, me).wait_send())
    over_tm(lambda d: copy_b(d, me).wait_send())
    over_tm(lambda d: copy_a(d, d).wait_recv())
    over_tm(lambda d: copy_b(d, d).wait_recv())


def unpack_kernel(tm, states, a_ref, b_ref, gx_ref, gdt_ref, gz_ref, gb_ref, gc_ref):
    length, width = gx_ref.shape
    frames = length // (S_DEV * tm)
    per = S_DEV * frames
    take_0 = unpack_matrix(row_of, 0, tm, per, frames, length)
    take_1 = unpack_matrix(row_of, 1, tm, per, frames, length)
    got_a = a_ref[...].reshape(tm * 2 * per, width)
    got_b = b_ref[...].reshape(tm * 2 * per, width)
    gdt_ref[...] = dot(take_0, got_a).astype(BF16)
    gz_ref[...] = dot(take_1, got_a).astype(BF16)
    gx_ref[...] = dot(take_0, got_b).astype(BF16)
    bc = dot(take_1, got_b[:, 0:128]).astype(BF16)
    row, lane = iotas((128, states))
    gb_ref[...] = dot(bc, ones_where(row == lane)).astype(BF16)
    gc_ref[...] = dot(bc, ones_where(row == lane + states)).astype(BF16)


def on_device(
    tm,
    chan,
    inner_x,
    gate_z,
    dt_raw,
    grad_out,
    input_b,
    output_c,
    conv_weight,
    conv_bias,
    decay_log,
    skip_gain,
):
    length, width = inner_x.shape
    states = input_b.shape[1]
    per = length // tm
    wide = width + 2 * states
    vmem = pl.BlockSpec(memory_space=pltpu.VMEM)
    rows = pltpu.VMEM((length, width), F32)
    block = (tm, 2 * per, width)
    sems = pltpu.SemaphoreType.DMA
    limit = 60 * 1024 * 1024
    scratch = [
        pltpu.VMEM((tm, 2 * per, wide), BF16),
        pltpu.VMEM(block, BF16),
        pltpu.VMEM((tm, 16, width), BF16),
        pltpu.VMEM((tm, 2 * per, wide), BF16),
        pltpu.VMEM(block, BF16),
        pltpu.VMEM((16, width), BF16),
        pltpu.VMEM((48, width), BF16),
        pltpu.VMEM((tm, 48, width), BF16),
        pltpu.VMEM((length, 128), F32),
        pltpu.VMEM((chan, length, 128), F32),
        pltpu.VMEM((8, width), F32),
        pltpu.VMEM((8, width), F32),
        pltpu.VMEM(block, BF16),
        pltpu.VMEM(block, BF16),
        pltpu.VMEM((length + 8, width), F32),
        *[rows] * 11,
        pltpu.VMEM((length + 8, width), F32),
        pltpu.VMEM((length * states, 256), F32),
        pltpu.VMEM((length * states, width), F32),
        pltpu.VMEM((3, BLK * states, width), BF16),
        sems((2, tm)),
        sems((2, tm)),
        sems((tm + 1,)),
        sems((2, tm)),
        sems((2, chan)),
        sems((2,)),
        sems((2, tm)),
        sems((2, tm)),
    ]
    out_a, out_b = pl.pallas_call(
        functools.partial(kernel, tm, chan),
        out_shape=[jax.ShapeDtypeStruct(block, BF16)] * 2,
        in_specs=[vmem] * 10,
        out_specs=[vmem] * 2,
        scratch_shapes=scratch,
        compiler_params=pltpu.CompilerParams(
            collective_id=0, has_side_effects=True, vmem_limit_bytes=limit
        ),
    )(
        inner_x,
        gate_z,
        dt_raw,
        grad_out,
        input_b,
        output_c,
        conv_weight,
        conv_bias.reshape(1, width),
        decay_log,
        skip_gain.reshape(1, width),
    )
    wide_out = jax.ShapeDtypeStruct((length, width), BF16)
    thin_out = jax.ShapeDtypeStruct((length, states), BF16)
    return pl.pallas_call(
        functools.partial(unpack_kernel, tm, states),
        out_shape=[wide_out, wide_out, wide_out, thin_out, thin_out],
        in_specs=[vmem] * 2,
        out_specs=[vmem] * 5,
        compiler_params=pltpu.CompilerParams(vmem_limit_bytes=limit),
    )(out_a, out_b)


def solution(mesh):
    return jax.shard_map(
        functools.partial(on_device, mesh.shape["tm"], mesh.shape["chan"]),
        mesh=mesh,
        in_specs=(
            P("tm", "chan"),
            P("tm", "chan"),
            P("tm", "chan"),
            P("tm", "chan"),
            P("tm", None),
            P("tm", None),
            P(None, "chan"),
            P("chan"),
            P(None, "chan"),
            P("chan"),
        ),
        out_specs=(P("tm", "chan"), P("tm", "chan"), P("tm", "chan"), P("tm", None), P("tm", None)),
        check_vma=False,
    )
```

```python
import functools

import jax
import jax.numpy as jnp
from jax import lax
from jax.experimental import pallas as pl
from jax.experimental.pallas import tpu as pltpu
from jax.sharding import PartitionSpec as P

S_DEV = 2
BLK = 16
F32 = jnp.float32
BF16 = jnp.bfloat16
MESH = pl.DeviceIdType.MESH


def log2(value):
    assert value & (value - 1) == 0
    return value.bit_length() - 1


def dot(left, right):
    return jnp.dot(left, right, preferred_element_type=F32)


def dot_t(left, right):
    return lax.dot_general(left, right, (((1,), (1,)), ((), ())), preferred_element_type=F32)


def iotas(shape):
    return lax.broadcasted_iota(jnp.int32, shape, 0), lax.broadcasted_iota(jnp.int32, shape, 1)


def ones_where(mask):
    return jnp.where(mask, 1.0, 0.0).astype(BF16)


def fields(packed, half, per, frames):
    partner = packed >> log2(2 * per)
    inside = packed & (2 * per - 1)
    rest = inside & (per - 1)
    spatial = rest >> log2(frames)
    frame = rest & (frames - 1)
    valid = (inside >> log2(per)) == half
    return partner, spatial, frame, valid


def row_of(packed, half, tm, per, frames):
    partner, spatial, frame, valid = fields(packed, half, per, frames)
    row = frame * (S_DEV * tm) + partner * S_DEV + spatial
    return jnp.where(valid, row, -1)


def place_of(packed, half, tm, per, frames):
    partner, spatial, frame, valid = fields(packed, half, per, frames)
    place = spatial * (frames * tm) + partner * frames + frame
    return jnp.where(valid, place, -1)


def pack_matrix(of, half, tm, per, frames, length):
    packed, row = iotas((tm * 2 * per, length))
    return ones_where(of(packed, half, tm, per, frames) == row)


def unpack_matrix(of, half, tm, per, frames, length):
    row, packed = iotas((length, tm * 2 * per))
    return ones_where(of(packed, half, tm, per, frames) == row)


def sigmoid(values):
    return 1.0 / (1.0 + jnp.exp(-values))


def silu_grad(values):
    sigm = sigmoid(values)
    return sigm * (1.0 + values * (1.0 - sigm))


def kernel(
    tm,
    chan,
    x_ref,
    z_ref,
    dt_ref,
    g_ref,
    b_ref,
    c_ref,
    w_ref,
    bias_ref,
    log_ref,
    skip_ref,
    out_a,
    out_b,
    send_1,
    send_2,
    send_h,
    recv_1,
    recv_2,
    recv_h,
    ends,
    ends_in,
    part,
    part_in,
    edge,
    edge_in,
    send_a,
    send_b,
    xpad,
    pre_s,
    conv_s,
    delta_s,
    u_s,
    dy_s,
    dt_s,
    z_s,
    g_s,
    y_s,
    w_s,
    d_s,
    gp_s,
    bc_s,
    fs_s,
    prod,
    sem_1,
    sem_2,
    sem_h,
    sem_e,
    sem_p,
    sem_g,
    sem_a,
    sem_b,
):
    me = lax.axis_index("tm")
    ch = lax.axis_index("chan")
    length, width = x_ref.shape
    states = b_ref.shape[0]
    taps = w_ref.shape[0]
    frames = length // (S_DEV * tm)
    per = S_DEV * frames
    wide = width + 2 * states
    base = width // 128 * 128

    def partner(k):
        return lax.rem(me + k, tm)

    def peer(k):
        return lax.rem(ch + k, chan)

    def over_tm(body):
        def step(k, carry):
            body(partner(k))
            return carry

        lax.fori_loop(1, tm, step, 0)

    def over_chan(body):
        for k in range(1, chan):
            body(peer(k))

    barrier = pltpu.get_barrier_semaphore()

    def greet(d):
        pl.semaphore_signal(barrier, inc=1, device_id={"tm": d}, device_id_type=MESH)

    def greet_peer(d):
        pl.semaphore_signal(barrier, inc=1, device_id={"chan": d}, device_id_type=MESH)

    over_tm(greet)
    over_chan(greet_peer)

    row, lane = iotas((width, wide))
    ex = ones_where(row == lane)
    row, lane = iotas((states, wide))
    eb = ones_where(lane == row + width)
    ec = ones_where(lane == row + width + states)
    x_ext = dot(x_ref[...], ex).astype(BF16)
    first = pack_matrix(row_of, 0, tm, per, frames, length)
    second = pack_matrix(row_of, 1, tm, per, frames, length)
    dt_ext = dot(dt_ref[...], ex).astype(BF16)
    b_rows = dot_t(first, b_ref[...]).astype(BF16)
    c_rows = dot_t(first, c_ref[...]).astype(BF16)
    one = dot(first, x_ext) + dot(second, dt_ext) + dot(b_rows, eb) + dot(c_rows, ec)
    send_1[...] = one.astype(BF16).reshape(tm, 2 * per, wide)
    packed, row = iotas((tm * 16, length))
    slot = packed & 15
    frame = slot - (8 - frames)
    source = frame * (S_DEV * tm) + (packed >> 4) * S_DEV - 1
    good = (frame >= 0) & (slot < 8) & (packed >= 16)
    halo = ones_where(jnp.where(good, source, -1) == row)
    send_h[...] = dot(halo, x_ref[...]).astype(BF16).reshape(tm, 16, width)

    def copy_tm(src, dst, sems, d, origin):
        return pltpu.make_async_remote_copy(
            src_ref=src,
            dst_ref=dst,
            send_sem=sems.at[0, d],
            recv_sem=sems.at[1, origin],
            device_id={"tm": d},
            device_id_type=MESH,
        )

    def copy_1(d, origin):
        return copy_tm(send_1.at[d], recv_1.at[origin], sem_1, d, origin)

    def copy_2(d, origin):
        return copy_tm(send_2.at[d], recv_2.at[origin], sem_2, d, origin)

    def copy_h(d):
        return pltpu.make_async_remote_copy(
            src_ref=send_h.at[d],
            dst_ref=recv_h,
            send_sem=sem_h.at[d],
            recv_sem=sem_h.at[tm],
            device_id={"tm": d},
            device_id_type=MESH,
        )

    def start_halo(d):
        @pl.when(me == tm - 1)
        def _():
            copy_h(d).start()

    pl.semaphore_wait(barrier, tm - 1 + chan - 1)
    over_tm(start_halo)
    over_tm(lambda d: copy_1(d, me).start())
    two = dot(first, z_ref[...]) + dot(second, g_ref[...])
    send_2[...] = two.astype(BF16).reshape(tm, 2 * per, width)
    over_tm(lambda d: copy_2(d, me).start())
    recv_1[me] = send_1[me]
    recv_2[me] = send_2[me]

    rate = -jnp.exp(log_ref[...])
    take_0 = unpack_matrix(place_of, 0, tm, per, frames, length)
    take_1 = unpack_matrix(place_of, 1, tm, per, frames, length)
    row, lane = iotas((BLK, BLK * states))
    sel = ones_where((lane >> log2(states)) == row)
    row, lane = iotas((BLK * states, BLK))
    spread = ones_where((row >> log2(states)) == lane)

    @pl.when(me == tm - 1)
    def _():
        recv_h[...] = send_h[me]

    @pl.when(me != tm - 1)
    def _():
        copy_h(me).wait_recv()

    over_tm(lambda d: copy_1(d, d).wait_recv())
    got_1 = recv_1[...].reshape(tm * 2 * per, wide)
    x_full = dot(take_0, got_1)
    dt_vals = dot(take_1, got_1[:, :width])
    xpad[0:8, :] = recv_h[...].astype(F32)[0:8]
    xpad[8:, :] = x_full[:, :width]
    tail = wide - base
    bc_bf = x_full[:, base:].astype(BF16)
    row, lane = iotas((BLK * states, tail))
    keep = ((lane - (width - base)) & (states - 1)) == (row & (states - 1))
    keep = keep & (lane >= width - base)
    row, lane = iotas((tail, 256))
    fan = ones_where(
        (row >= width - base)
        & (((row - (width - base)) >> log2(states)) == (lane >> 7))
    )
    for block in range(length // BLK):
        rows = dot(spread, bc_bf[block * BLK : (block + 1) * BLK])
        rows = jnp.where(keep, rows, 0.0).astype(BF16)
        bc_s[block * BLK * states : (block + 1) * BLK * states, :] = dot(rows, fan)

    dt_s[...] = dt_vals
    deltas = jnp.maximum(dt_vals, 0.0) + jnp.log(1.0 + jnp.exp(-jnp.abs(dt_vals)))
    delta_s[...] = deltas
    pre = bias_ref[...].reshape(1, width) + w_ref[0:1, :] * xpad[8 - taps + 1 : 8 - taps + 1 + length, :]
    for k in range(1, taps):
        pre = pre + w_ref[k : k + 1, :] * xpad[8 - taps + 1 + k : 8 - taps + 1 + k + length, :]
    pre_s[...] = pre
    conv = pre * sigmoid(pre)
    conv_s[...] = conv
    u_s[...] = deltas * conv
    total = jnp.sum(deltas, axis=0, keepdims=True)

    over_tm(lambda d: copy_2(d, d).wait_recv())
    got_2 = recv_2[...].reshape(tm * 2 * per, width)
    z_vals = dot(take_0, got_2)
    g_vals = dot(take_1, got_2)
    z_s[...] = z_vals
    g_s[...] = g_vals
    dy_s[...] = (g_vals * (z_vals * sigmoid(z_vals))).astype(BF16).astype(F32)

    def over_lanes(tile):
        return jnp.concatenate([tile] * (width // 128) + [tile[:, : width % 128]], axis=1)

    def b_at(q):
        return over_lanes(bc_s[pl.ds(pl.multiple_of(q * states, states), states), 0:128])

    def c_at(q):
        return over_lanes(bc_s[pl.ds(pl.multiple_of(q * states, states), states), 128:256])

    zero = jnp.zeros((states, width), F32)

    def local(i, carry):
        state, back = carry
        up = pl.multiple_of(i * 8, 8)
        down = pl.multiple_of(length - 8 - i * 8, 8)
        d_up, u_up = delta_s[pl.ds(up, 8), :], u_s[pl.ds(up, 8), :]
        d_dn, y_dn = delta_s[pl.ds(down, 8), :], dy_s[pl.ds(down, 8), :]
        for j in range(8):
            state = jnp.exp(d_up[j : j + 1] * rate) * state + u_up[j : j + 1] * b_at(up + j)
            m = 7 - j
            back = jnp.exp(d_dn[m : m + 1] * rate) * (y_dn[m : m + 1] * c_at(down + m) + back)
        return state, back

    end, back_end = lax.fori_loop(0, length // 8, local, (zero, zero))
    row = lax.broadcasted_iota(jnp.int32, (16, width), 0)
    high = total.astype(BF16).astype(F32)
    sums = jnp.where(row == 0, high, jnp.where(row == 1, total - high, 0.0))
    ends[0:16, :] = end.astype(BF16)
    ends[16:32, :] = sums.astype(BF16)
    ends[32:48, :] = back_end.astype(BF16)

    def copy_up(d, origin):
        return copy_tm(ends.at[0:32], ends_in.at[origin, 0:32], sem_e, d, origin)

    def copy_down(d, origin):
        return copy_tm(ends.at[16:48], ends_in.at[origin, 16:48], sem_e, d, origin)

    def send_end(d):
        @pl.when(d > me)
        def _():
            copy_up(d, me).start()

        @pl.when(d < me)
        def _():
            copy_down(d, me).start()

    over_tm(send_end)

    def through(source):
        pair = ends_in[source, 16:32, :].astype(F32)
        return jnp.exp(rate * (pair[0:1] + pair[1:2]))

    def enter_up(source, state):
        copy_up(source, source).wait_recv()
        return through(source) * state + ends_in[source, 0:16, :].astype(F32)

    def enter_down(turn, back):
        source = tm - 1 - turn
        copy_down(source, source).wait_recv()
        return through(source) * back + ends_in[source, 32:48, :].astype(F32)

    state_in = lax.fori_loop(0, me, enter_up, zero)
    back_in = lax.fori_loop(0, tm - 1 - me, enter_down, zero)

    row, lane = iotas((BLK * states, 128))
    at_b = lane == (row & (states - 1))
    at_c = lane == (row & (states - 1)) + states
    ones = jnp.ones((width, 128), BF16)
    skip = skip_ref[...].reshape(1, width)

    def picked(product, where):
        sums = jnp.where(where, dot(product, ones), 0.0)
        high = sums.astype(BF16)
        low = (sums - high.astype(F32)).astype(BF16)
        return dot(sel, high) + dot(sel, low)

    def forward(i, state):
        start = pl.multiple_of(i * BLK, BLK)
        here = pl.ds(start, BLK)
        d_blk, u_blk, y_blk = delta_s[here, :], u_s[here, :], dy_s[here, :]
        for j in range(BLK):
            kept = jnp.exp(d_blk[j : j + 1] * rate) * state
            state = kept + u_blk[j : j + 1] * b_at(start + j)
            fs_s[pl.ds(pl.multiple_of((start + j) * states, states), states), :] = kept
            prod[0, j * states : (j + 1) * states, :] = (c_at(start + j) * state).astype(BF16)
            prod[1, j * states : (j + 1) * states, :] = (y_blk[j : j + 1] * state).astype(BF16)
        y_s[here, :] = dot(sel, prod[0]) + skip * conv_s[here, :]
        part[here, :] = picked(prod[1], at_c)
        return state

    lax.fori_loop(0, length // BLK, forward, state_in)

    def backward(turn, back):
        start = pl.multiple_of(length - BLK - turn * BLK, BLK)
        here = pl.ds(start, BLK)
        d_blk, u_blk, y_blk = delta_s[here, :], u_s[here, :], dy_s[here, :]
        for j in reversed(range(BLK)):
            adjoint = y_blk[j : j + 1] * c_at(start + j) + back
            back = jnp.exp(d_blk[j : j + 1] * rate) * adjoint
            kept = fs_s[pl.ds(pl.multiple_of((start + j) * states, states), states), :]
            rows = slice(j * states, (j + 1) * states)
            prod[0, rows, :] = (adjoint * b_at(start + j)).astype(BF16)
            prod[1, rows, :] = (adjoint * u_blk[j : j + 1]).astype(BF16)
            prod[2, rows, :] = (adjoint * rate * kept).astype(BF16)
        w_s[here, :] = dot(sel, prod[0])
        d_s[here, :] = dot(sel, prod[2])
        part[here, :] = part[here, :] + picked(prod[1], at_b)
        return back

    lax.fori_loop(0, length // BLK, backward, back_in)

    def copy_part(d, origin):
        return pltpu.make_async_remote_copy(
            src_ref=part,
            dst_ref=part_in.at[origin],
            send_sem=sem_p.at[0, d],
            recv_sem=sem_p.at[1, origin],
            device_id={"chan": d},
            device_id_type=MESH,
        )

    over_chan(lambda d: copy_part(d, ch).start())
    deltas = delta_s[...]
    weighted = w_s[...]
    grad_pre = (skip * dy_s[...] + deltas * weighted) * silu_grad(pre_s[...])
    gp_s[0:length, :] = grad_pre
    edge[...] = grad_pre[0:8]

    def copy_edge(d):
        return pltpu.make_async_remote_copy(
            src_ref=edge,
            dst_ref=edge_in,
            send_sem=sem_g.at[0],
            recv_sem=sem_g.at[1],
            device_id={"tm": d},
            device_id_type=MESH,
        )

    before = jnp.maximum(me - 1, 0)

    @pl.when(me > 0)
    def _():
        copy_edge(before).start()

    give_0 = pack_matrix(place_of, 0, tm, per, frames, length)
    give_1 = pack_matrix(place_of, 1, tm, per, frames, length)
    grad_dt = ((d_s[...] + conv_s[...] * weighted) * sigmoid(dt_s[...])).astype(BF16)
    seq_y = y_s[...].astype(BF16).astype(F32)
    grad_z = (g_s[...] * seq_y * silu_grad(z_s[...])).astype(BF16)
    both = (dot(give_0, grad_dt) + dot(give_1, grad_z)).astype(BF16)
    send_a[...] = both.reshape(tm, 2 * per, width)

    def copy_a(d, origin):
        return copy_tm(send_a.at[d], out_a.at[origin], sem_a, d, origin)

    def copy_b(d, origin):
        return copy_tm(send_b.at[d], out_b.at[origin], sem_b, d, origin)

    over_tm(lambda d: copy_a(d, me).start())
    out_a[me] = send_a[me]

    @pl.when(me < tm - 1)
    def _():
        copy_edge(before).wait_recv()
        gp_s[length:, :] = edge_in[...]

    @pl.when(me == tm - 1)
    def _():
        gp_s[length:, :] = jnp.zeros((8, width), F32)

    grad_x = w_ref[0:1, :] * gp_s[taps - 1 : taps - 1 + length, :]
    for k in range(1, taps):
        grad_x = grad_x + w_ref[k : k + 1, :] * gp_s[taps - 1 - k : taps - 1 - k + length, :]
    x_part = dot(give_0, grad_x.astype(BF16))
    over_chan(lambda d: copy_part(d, d).wait_recv())
    part_in[ch] = part[...]
    bc = part_in[0]
    for k in range(1, chan):
        bc = bc + part_in[k]
    bc = jnp.concatenate([bc.astype(BF16), jnp.zeros((length, width - 128), BF16)], axis=1)
    send_b[...] = (x_part + dot(give_1, bc)).astype(BF16).reshape(tm, 2 * per, width)
    over_tm(lambda d: copy_b(d, me).start())
    out_b[me] = send_b[me]

    over_tm(lambda d: copy_1(d, me).wait_send())
    over_tm(lambda d: copy_2(d, me).wait_send())

    def end_halo(d):
        @pl.when(me == tm - 1)
        def _():
            copy_h(d).wait_send()

    over_tm(end_halo)

    def end_ends(d):
        @pl.when(d > me)
        def _():
            copy_up(d, me).wait_send()

        @pl.when(d < me)
        def _():
            copy_down(d, me).wait_send()

    over_tm(end_ends)
    over_chan(lambda d: copy_part(d, ch).wait_send())

    @pl.when(me > 0)
    def _():
        copy_edge(before).wait_send()

    over_tm(lambda d: copy_a(d, me).wait_send())
    over_tm(lambda d: copy_b(d, me).wait_send())
    over_tm(lambda d: copy_a(d, d).wait_recv())
    over_tm(lambda d: copy_b(d, d).wait_recv())


def unpack_kernel(tm, states, a_ref, b_ref, gx_ref, gdt_ref, gz_ref, gb_ref, gc_ref):
    length, width = gx_ref.shape
    frames = length // (S_DEV * tm)
    per = S_DEV * frames
    take_0 = unpack_matrix(row_of, 0, tm, per, frames, length)
    take_1 = unpack_matrix(row_of, 1, tm, per, frames, length)
    got_a = a_ref[...].reshape(tm * 2 * per, width)
    got_b = b_ref[...].reshape(tm * 2 * per, width)
    gdt_ref[...] = dot(take_0, got_a).astype(BF16)
    gz_ref[...] = dot(take_1, got_a).astype(BF16)
    gx_ref[...] = dot(take_0, got_b).astype(BF16)
    bc = dot(take_1, got_b[:, 0:128]).astype(BF16)
    row, lane = iotas((states, 128))
    gb_ref[...] = dot_t(ones_where(row == lane), bc).astype(BF16)
    gc_ref[...] = dot_t(ones_where(row + states == lane), bc).astype(BF16)


def on_device(
    tm,
    chan,
    inner_x,
    gate_z,
    dt_raw,
    grad_out,
    input_b,
    output_c,
    conv_weight,
    conv_bias,
    decay_log,
    skip_gain,
):
    length, width = inner_x.shape
    states = input_b.shape[1]
    per = length // tm
    wide = width + 2 * states
    vmem = pl.BlockSpec(memory_space=pltpu.VMEM)
    rows = pltpu.VMEM((length, width), F32)
    block = (tm, 2 * per, width)
    sems = pltpu.SemaphoreType.DMA
    limit = 60 * 1024 * 1024
    scratch = [
        pltpu.VMEM((tm, 2 * per, wide), BF16),
        pltpu.VMEM(block, BF16),
        pltpu.VMEM((tm, 16, width), BF16),
        pltpu.VMEM((tm, 2 * per, wide), BF16),
        pltpu.VMEM(block, BF16),
        pltpu.VMEM((16, width), BF16),
        pltpu.VMEM((48, width), BF16),
        pltpu.VMEM((tm, 48, width), BF16),
        pltpu.VMEM((length, 128), F32),
        pltpu.VMEM((chan, length, 128), F32),
        pltpu.VMEM((8, width), F32),
        pltpu.VMEM((8, width), F32),
        pltpu.VMEM(block, BF16),
        pltpu.VMEM(block, BF16),
        pltpu.VMEM((length + 8, width), F32),
        *[rows] * 11,
        pltpu.VMEM((length + 8, width), F32),
        pltpu.VMEM((length * states, 256), F32),
        pltpu.VMEM((length * states, width), F32),
        pltpu.VMEM((3, BLK * states, width), BF16),
        sems((2, tm)),
        sems((2, tm)),
        sems((tm + 1,)),
        sems((2, tm)),
        sems((2, chan)),
        sems((2,)),
        sems((2, tm)),
        sems((2, tm)),
    ]
    out_a, out_b = pl.pallas_call(
        functools.partial(kernel, tm, chan),
        out_shape=[jax.ShapeDtypeStruct(block, BF16)] * 2,
        in_specs=[vmem] * 10,
        out_specs=[vmem] * 2,
        scratch_shapes=scratch,
        compiler_params=pltpu.CompilerParams(
            collective_id=0, has_side_effects=True, vmem_limit_bytes=limit
        ),
    )(
        inner_x,
        gate_z,
        dt_raw,
        grad_out,
        input_b.T,
        output_c.T,
        conv_weight,
        conv_bias,
        decay_log,
        skip_gain,
    )
    wide_out = jax.ShapeDtypeStruct((length, width), BF16)
    thin_out = jax.ShapeDtypeStruct((states, length), BF16)
    gx, gdt, gz, gb, gc = pl.pallas_call(
        functools.partial(unpack_kernel, tm, states),
        out_shape=[wide_out, wide_out, wide_out, thin_out, thin_out],
        in_specs=[vmem] * 2,
        out_specs=[vmem] * 5,
        compiler_params=pltpu.CompilerParams(vmem_limit_bytes=limit),
    )(out_a, out_b)
    return gx, gdt, gz, gb.T, gc.T


def solution(mesh):
    return jax.shard_map(
        functools.partial(on_device, mesh.shape["tm"], mesh.shape["chan"]),
        mesh=mesh,
        in_specs=(
            P("tm", "chan"),
            P("tm", "chan"),
            P("tm", "chan"),
            P("tm", "chan"),
            P("tm", None),
            P("tm", None),
            P(None, "chan"),
            P("chan"),
            P(None, "chan"),
            P("chan"),
        ),
        out_specs=(P("tm", "chan"), P("tm", "chan"), P("tm", "chan"), P("tm", None), P("tm", None)),
        check_vma=False,
    )
```

```python
import functools

import jax
import jax.numpy as jnp
from jax import lax
from jax.experimental import pallas as pl
from jax.experimental.pallas import tpu as pltpu
from jax.sharding import PartitionSpec as P

S_DEV = 2
BLK = 16
F32 = jnp.float32
BF16 = jnp.bfloat16
MESH = pl.DeviceIdType.MESH


def log2(value):
    assert value & (value - 1) == 0
    return value.bit_length() - 1


def dot(left, right):
    return jnp.dot(left, right, preferred_element_type=F32)


def dot_t(left, right):
    return lax.dot_general(left, right, (((1,), (1,)), ((), ())), preferred_element_type=F32)


def iotas(shape):
    return lax.broadcasted_iota(jnp.int32, shape, 0), lax.broadcasted_iota(jnp.int32, shape, 1)


def ones_where(mask):
    return jnp.where(mask, 1.0, 0.0).astype(BF16)


def fields(packed, half, per, frames):
    partner = packed >> log2(2 * per)
    inside = packed & (2 * per - 1)
    rest = inside & (per - 1)
    spatial = rest >> log2(frames)
    frame = rest & (frames - 1)
    valid = (inside >> log2(per)) == half
    return partner, spatial, frame, valid


def row_of(packed, half, tm, per, frames):
    partner, spatial, frame, valid = fields(packed, half, per, frames)
    row = frame * (S_DEV * tm) + partner * S_DEV + spatial
    return jnp.where(valid, row, -1)


def place_of(packed, half, tm, per, frames):
    partner, spatial, frame, valid = fields(packed, half, per, frames)
    place = spatial * (frames * tm) + partner * frames + frame
    return jnp.where(valid, place, -1)


def pack_matrix(of, half, tm, per, frames, length):
    packed, row = iotas((tm * 2 * per, length))
    return ones_where(of(packed, half, tm, per, frames) == row)


def unpack_matrix(of, half, tm, per, frames, length):
    row, packed = iotas((length, tm * 2 * per))
    return ones_where(of(packed, half, tm, per, frames) == row)


def sigmoid(values):
    return 1.0 / (1.0 + jnp.exp(-values))


def silu_grad(values):
    sigm = sigmoid(values)
    return sigm * (1.0 + values * (1.0 - sigm))


def kernel(
    tm,
    chan,
    x_any,
    z_any,
    dt_any,
    g_any,
    b_any,
    c_any,
    w_any,
    bias_any,
    log_any,
    skip_any,
    out_a,
    out_b,
    out_p,
    x_ref,
    z_ref,
    dt_ref,
    g_ref,
    b_ref,
    c_ref,
    w_ref,
    bias_ref,
    log_ref,
    skip_ref,
    send_1,
    send_2,
    send_h,
    recv_1,
    recv_2,
    recv_h,
    end_up,
    end_down,
    ends_in,
    tot,
    tot_in,
    part,
    send_p,
    send_a,
    send_b,
    xpad,
    pre_s,
    conv_s,
    delta_s,
    u_s,
    dy_s,
    dt_s,
    z_s,
    g_s,
    y_s,
    w_s,
    d_s,
    gp_s,
    bc_s,
    fs_s,
    prod,
    sem_in,
    sem_1,
    sem_2,
    sem_h,
    sem_e,
    sem_t,
    sem_p,
    sem_a,
    sem_b,
):
    me = lax.axis_index("tm")
    ch = lax.axis_index("chan")
    length, width = x_ref.shape
    states = b_ref.shape[0]
    taps = w_ref.shape[0]
    frames = length // (S_DEV * tm)
    per = S_DEV * frames
    wide = width + 2 * states
    base = width // 128 * 128

    def over_tm(body):
        def step(k, carry):
            down = tm - 1 - k
            down = jnp.where(down > me, down, down - 1)
            up = jnp.where(k < me, k, k + 1)
            body(jnp.where(me < tm // 2, down, up))
            return carry

        lax.fori_loop(0, tm - 1, step, 0)

    def over_all(body):
        for j in range(chan):
            c = lax.rem(ch + j, chan)

            def step(k, carry):
                body(lax.rem(me + k, tm), c)
                return carry

            lax.fori_loop(0 if j else 1, tm, step, 0)

    barrier = pltpu.get_barrier_semaphore()

    def greet(d, c):
        pl.semaphore_signal(
            barrier, inc=1, device_id={"tm": d, "chan": c}, device_id_type=MESH
        )

    over_all(greet)
    outside = (
        x_any, z_any, dt_any, g_any, b_any, c_any, w_any, bias_any, log_any, skip_any
    )
    inside = (x_ref, z_ref, dt_ref, g_ref, b_ref, c_ref, w_ref, bias_ref, log_ref, skip_ref)
    loads = [
        pltpu.make_async_copy(source, target, sem_in.at[k])
        for k, (source, target) in enumerate(zip(outside, inside))
    ]
    for load in loads:
        load.start()
    for load in loads:
        load.wait()

    row, lane = iotas((width, wide))
    ex = ones_where(row == lane)
    row, lane = iotas((states, wide))
    eb = ones_where(lane == row + width)
    ec = ones_where(lane == row + width + states)
    x_ext = dot(x_ref[...], ex).astype(BF16)
    first = pack_matrix(row_of, 0, tm, per, frames, length)
    second = pack_matrix(row_of, 1, tm, per, frames, length)
    dt_ext = dot(dt_ref[...], ex).astype(BF16)
    b_rows = dot_t(first, b_ref[...]).astype(BF16)
    c_rows = dot_t(first, c_ref[...]).astype(BF16)
    one = dot(first, x_ext) + dot(second, dt_ext) + dot(b_rows, eb) + dot(c_rows, ec)
    send_1[...] = one.astype(BF16).reshape(tm, 2 * per, wide)
    packed, row = iotas((tm * 16, length))
    slot = packed & 15
    frame = slot - (8 - frames)
    source = frame * (S_DEV * tm) + (packed >> 4) * S_DEV - 1
    good = (frame >= 0) & (slot < 8) & (packed >= 16)
    halo = ones_where(jnp.where(good, source, -1) == row)
    send_h[...] = dot(halo, x_ref[...]).astype(BF16).reshape(tm, 16, width)

    def copy_tm(src, dst, sems, d, origin):
        return pltpu.make_async_remote_copy(
            src_ref=src,
            dst_ref=dst,
            send_sem=sems.at[0, d],
            recv_sem=sems.at[1, origin],
            device_id={"tm": d},
            device_id_type=MESH,
        )

    def copy_1(d, origin):
        return copy_tm(send_1.at[d], recv_1.at[origin], sem_1, d, origin)

    def copy_2(d, origin):
        return copy_tm(send_2.at[d], recv_2.at[origin], sem_2, d, origin)

    def copy_h(d):
        return pltpu.make_async_remote_copy(
            src_ref=send_h.at[d],
            dst_ref=recv_h,
            send_sem=sem_h.at[d],
            recv_sem=sem_h.at[tm],
            device_id={"tm": d},
            device_id_type=MESH,
        )

    def start_halo(d):
        @pl.when(me == tm - 1)
        def _():
            copy_h(d).start()

    pl.semaphore_wait(barrier, tm * chan - 1)
    over_tm(start_halo)
    over_tm(lambda d: copy_1(d, me).start())
    two = dot(first, z_ref[...]) + dot(second, g_ref[...])
    send_2[...] = two.astype(BF16).reshape(tm, 2 * per, width)
    over_tm(lambda d: copy_2(d, me).start())
    recv_1[me] = send_1[me]
    recv_2[me] = send_2[me]

    rate = -jnp.exp(log_ref[...])
    take_0 = unpack_matrix(place_of, 0, tm, per, frames, length)
    take_1 = unpack_matrix(place_of, 1, tm, per, frames, length)
    row, lane = iotas((BLK, BLK * states))
    sel = ones_where((lane >> log2(states)) == row)
    row, lane = iotas((BLK * states, BLK))
    spread = ones_where((row >> log2(states)) == lane)

    @pl.when(me == tm - 1)
    def _():
        recv_h[...] = send_h[me]

    @pl.when(me != tm - 1)
    def _():
        copy_h(me).wait_recv()

    over_tm(lambda d: copy_1(d, d).wait_recv())
    got_1 = recv_1[...].reshape(tm * 2 * per, wide)
    x_full = dot(take_0, got_1)
    dt_vals = dot(take_1, got_1[:, :width])
    xpad[0:8, :] = recv_h[...].astype(F32)[0:8]
    xpad[8:, :] = x_full[:, :width]
    tail = wide - base
    bc_bf = x_full[:, base:].astype(BF16)
    row, lane = iotas((BLK * states, tail))
    keep = ((lane - (width - base)) & (states - 1)) == (row & (states - 1))
    keep = keep & (lane >= width - base)
    row, lane = iotas((tail, 256))
    fan = ones_where(
        (row >= width - base)
        & (((row - (width - base)) >> log2(states)) == (lane >> 7))
    )
    for block in range(length // BLK):
        rows = dot(spread, bc_bf[block * BLK : (block + 1) * BLK])
        rows = jnp.where(keep, rows, 0.0).astype(BF16)
        bc_s[block * BLK * states : (block + 1) * BLK * states, :] = dot(rows, fan)

    dt_s[...] = dt_vals
    deltas = jnp.maximum(dt_vals, 0.0) + jnp.log(1.0 + jnp.exp(-jnp.abs(dt_vals)))
    delta_s[...] = deltas
    pre = bias_ref[...].reshape(1, width) + w_ref[0:1, :] * xpad[8 - taps + 1 : 8 - taps + 1 + length, :]
    for k in range(1, taps):
        pre = pre + w_ref[k : k + 1, :] * xpad[8 - taps + 1 + k : 8 - taps + 1 + k + length, :]
    pre_s[...] = pre
    conv = pre * sigmoid(pre)
    conv_s[...] = conv
    u_s[...] = deltas * conv
    total = jnp.sum(deltas, axis=0, keepdims=True)
    padded = jnp.concatenate([total, jnp.zeros((1, 128 - width % 128), F32)], axis=1)
    lines = [padded[:, k : k + 128] for k in range(0, width, 128)]
    tot[...] = jnp.concatenate(lines + [jnp.zeros((8 - len(lines), 128), F32)], axis=0)

    def copy_tot(d, origin):
        return copy_tm(tot, tot_in.at[origin], sem_t, d, origin)

    over_tm(lambda d: copy_tot(d, me).start())

    over_tm(lambda d: copy_2(d, d).wait_recv())
    got_2 = recv_2[...].reshape(tm * 2 * per, width)
    z_vals = dot(take_0, got_2)
    g_vals = dot(take_1, got_2)
    z_s[...] = z_vals
    g_s[...] = g_vals
    dy_s[...] = (g_vals * (z_vals * sigmoid(z_vals))).astype(BF16).astype(F32)

    def over_lanes(tile):
        return jnp.concatenate([tile] * (width // 128) + [tile[:, : width % 128]], axis=1)

    def b_at(q):
        return over_lanes(bc_s[pl.ds(pl.multiple_of(q * states, states), states), 0:128])

    def c_at(q):
        return over_lanes(bc_s[pl.ds(pl.multiple_of(q * states, states), states), 128:256])

    zero = jnp.zeros((states, width), F32)

    def local(i, carry):
        state, back = carry
        up = pl.multiple_of(i * 8, 8)
        down = pl.multiple_of(length - 8 - i * 8, 8)
        d_up, u_up = delta_s[pl.ds(up, 8), :], u_s[pl.ds(up, 8), :]
        d_dn, y_dn = delta_s[pl.ds(down, 8), :], dy_s[pl.ds(down, 8), :]
        for j in range(8):
            state = jnp.exp(d_up[j : j + 1] * rate) * state + u_up[j : j + 1] * b_at(up + j)
            m = 7 - j
            back = jnp.exp(d_dn[m : m + 1] * rate) * (y_dn[m : m + 1] * c_at(down + m) + back)
        return state, back

    end, back_end = lax.fori_loop(0, length // 8, local, (zero, zero))
    end_up[...] = end.astype(BF16)
    end_down[...] = back_end.astype(BF16)

    def copy_up(d, origin):
        return copy_tm(end_up, ends_in.at[origin], sem_e, d, origin)

    def copy_down(d, origin):
        return copy_tm(end_down, ends_in.at[origin], sem_e, d, origin)

    def send_end(d):
        @pl.when(d > me)
        def _():
            copy_up(d, me).start()

        @pl.when(d < me)
        def _():
            copy_down(d, me).start()

    over_tm(send_end)

    def through(source):
        lines = tot_in[source]
        pieces = [lines[k : k + 1, : min(128, width - 128 * k)] for k in range(-(-width // 128))]
        return jnp.exp(rate * jnp.concatenate(pieces, axis=1))

    over_tm(lambda d: copy_tot(d, d).wait_recv())

    def enter_up(source, state):
        copy_up(source, source).wait_recv()
        return through(source) * state + ends_in[source].astype(F32)

    def enter_down(turn, back):
        source = tm - 1 - turn
        copy_down(source, source).wait_recv()
        return through(source) * back + ends_in[source].astype(F32)

    state_in = lax.fori_loop(0, me, enter_up, zero)
    back_in = lax.fori_loop(0, tm - 1 - me, enter_down, zero)

    row, lane = iotas((BLK * states, 128))
    at_b = lane == (row & (states - 1))
    at_c = lane == (row & (states - 1)) + states
    ones = jnp.ones((width, 128), BF16)
    skip = skip_ref[...].reshape(1, width)

    def picked(product, where):
        sums = jnp.where(where, dot(product, ones), 0.0)
        high = sums.astype(BF16)
        low = (sums - high.astype(F32)).astype(BF16)
        return dot(sel, high) + dot(sel, low)

    def forward(i, state):
        start = pl.multiple_of(i * BLK, BLK)
        here = pl.ds(start, BLK)
        d_blk, u_blk, y_blk = delta_s[here, :], u_s[here, :], dy_s[here, :]
        for j in range(BLK):
            kept = jnp.exp(d_blk[j : j + 1] * rate) * state
            state = kept + u_blk[j : j + 1] * b_at(start + j)
            fs_s[pl.ds(pl.multiple_of((start + j) * states, states), states), :] = kept
            prod[0, j * states : (j + 1) * states, :] = (c_at(start + j) * state).astype(BF16)
            prod[1, j * states : (j + 1) * states, :] = (y_blk[j : j + 1] * state).astype(BF16)
        y_s[here, :] = dot(sel, prod[0]) + skip * conv_s[here, :]
        part[here, :] = picked(prod[1], at_c)
        return state

    lax.fori_loop(0, length // BLK, forward, state_in)

    def backward(turn, back):
        start = pl.multiple_of(length - BLK - turn * BLK, BLK)
        here = pl.ds(start, BLK)
        d_blk, u_blk, y_blk = delta_s[here, :], u_s[here, :], dy_s[here, :]
        for j in reversed(range(BLK)):
            adjoint = y_blk[j : j + 1] * c_at(start + j) + back
            back = jnp.exp(d_blk[j : j + 1] * rate) * adjoint
            kept = fs_s[pl.ds(pl.multiple_of((start + j) * states, states), states), :]
            rows = slice(j * states, (j + 1) * states)
            prod[0, rows, :] = (adjoint * b_at(start + j)).astype(BF16)
            prod[1, rows, :] = (adjoint * u_blk[j : j + 1]).astype(BF16)
            prod[2, rows, :] = (adjoint * rate * kept).astype(BF16)
        w_s[here, :] = dot(sel, prod[0])
        d_s[here, :] = dot(sel, prod[2])
        part[here, :] = part[here, :] + picked(prod[1], at_b)
        return back

    lax.fori_loop(0, length // BLK, backward, back_in)

    def copy_a(d, origin):
        return copy_tm(send_a.at[d], out_a.at[origin], sem_a, d, origin)

    def copy_b(d, origin):
        return copy_tm(send_b.at[d], out_b.at[origin], sem_b, d, origin)

    def copy_p(d, c, from_d, from_c):
        return pltpu.make_async_remote_copy(
            src_ref=send_p.at[d],
            dst_ref=out_p.at[from_c, from_d],
            send_sem=sem_p.at[0, c, d],
            recv_sem=sem_p.at[1, from_c, from_d],
            device_id={"tm": d, "chan": c},
            device_id_type=MESH,
        )

    packed, row = iotas((tm * per, length))
    place = ((packed & (per - 1)) >> log2(frames)) * (frames * tm)
    place = place + (packed >> log2(per)) * frames + (packed & (frames - 1))
    give = ones_where(place == row)
    sums = part[...]
    high = sums.astype(BF16)
    low = (sums - high.astype(F32)).astype(BF16)
    send_p[...] = (dot(give, high) + dot(give, low)).reshape(tm, per, 128)
    over_all(lambda d, c: copy_p(d, c, me, ch).start())

    deltas = delta_s[...]
    weighted = w_s[...]
    grad_pre = (skip * dy_s[...] + deltas * weighted) * silu_grad(pre_s[...])
    gp_s[0:8, :] = jnp.zeros((8, width), F32)
    gp_s[8 : 8 + length, :] = grad_pre
    gp_s[8 + length :, :] = jnp.zeros((8, width), F32)
    grad_x = w_ref[0:1, :] * gp_s[taps - 1 : taps + 7 + length, :]
    for k in range(1, taps):
        grad_x = grad_x + w_ref[k : k + 1, :] * gp_s[taps - 1 - k : taps + 7 - k + length, :]
    packed, row = iotas((tm * 2 * per, length + 8))
    place = place_of(packed, 0, tm, per, frames)
    slot = packed & (2 * per - 1)
    spill = (packed >= (tm - 1) * 2 * per) & (slot > 2 * per - taps)
    column = jnp.where(place >= 0, place + 8, jnp.where(spill, slot + 8 - 2 * per, -1))
    both = dot(ones_where(column == row), grad_x.astype(BF16)).astype(BF16)
    send_b[...] = both.reshape(tm, 2 * per, width)
    over_tm(lambda d: copy_b(d, me).start())

    give_0 = pack_matrix(place_of, 0, tm, per, frames, length)
    give_1 = pack_matrix(place_of, 1, tm, per, frames, length)
    grad_dt = ((d_s[...] + conv_s[...] * weighted) * sigmoid(dt_s[...])).astype(BF16)
    seq_y = y_s[...].astype(BF16).astype(F32)
    grad_z = (g_s[...] * seq_y * silu_grad(z_s[...])).astype(BF16)
    both = (dot(give_0, grad_dt) + dot(give_1, grad_z)).astype(BF16)
    send_a[...] = both.reshape(tm, 2 * per, width)
    over_tm(lambda d: copy_a(d, me).start())
    out_p[ch, me] = send_p[me]
    out_b[me] = send_b[me]
    out_a[me] = send_a[me]

    over_tm(lambda d: copy_1(d, me).wait_send())
    over_tm(lambda d: copy_2(d, me).wait_send())

    def end_halo(d):
        @pl.when(me == tm - 1)
        def _():
            copy_h(d).wait_send()

    over_tm(end_halo)

    def end_ends(d):
        @pl.when(d > me)
        def _():
            copy_up(d, me).wait_send()

        @pl.when(d < me)
        def _():
            copy_down(d, me).wait_send()

    over_tm(end_ends)
    over_tm(lambda d: copy_tot(d, me).wait_send())
    over_all(lambda d, c: copy_p(d, c, me, ch).wait_send())
    over_tm(lambda d: copy_a(d, me).wait_send())
    over_tm(lambda d: copy_b(d, me).wait_send())
    over_tm(lambda d: copy_a(d, d).wait_recv())
    over_tm(lambda d: copy_b(d, d).wait_recv())
    over_all(lambda d, c: copy_p(d, c, d, c).wait_recv())


def unpack_kernel(tm, states, taps, a_ref, b_ref, p_ref, gx_ref, gdt_ref, gz_ref, gb_ref, gc_ref):
    length, width = gx_ref.shape
    frames = length // (S_DEV * tm)
    per = S_DEV * frames
    take_0 = unpack_matrix(row_of, 0, tm, per, frames, length)
    take_1 = unpack_matrix(row_of, 1, tm, per, frames, length)
    row, packed = iotas((length, tm * 2 * per))
    slot = packed & (2 * per - 1)
    owner = (packed >> log2(2 * per)) - 1
    frame = slot - 2 * per + frames
    added = frame * (S_DEV * tm) + owner * S_DEV + S_DEV - 1
    added = jnp.where((slot > 2 * per - taps) & (owner >= 0), added, -1)
    both = ones_where((row_of(packed, 0, tm, per, frames) == row) | (added == row))
    got_a = a_ref[...].reshape(tm * 2 * per, width)
    got_b = b_ref[...].reshape(tm * 2 * per, width)
    gdt_ref[...] = dot(take_0, got_a).astype(BF16)
    gz_ref[...] = dot(take_1, got_a).astype(BF16)
    gx_ref[...] = dot(both, got_b).astype(BF16)
    sums = p_ref[0]
    for k in range(1, p_ref.shape[0]):
        sums = sums + p_ref[k]
    row, packed = iotas((length, tm * per))
    source = (packed & (frames - 1)) * (S_DEV * tm) + (packed >> log2(per)) * S_DEV
    source = source + ((packed & (per - 1)) >> log2(frames))
    thin = sums.reshape(tm * per, 128).astype(BF16)
    bc = dot(ones_where(source == row), thin).astype(BF16)
    row, lane = iotas((states, 128))
    gb_ref[...] = dot_t(ones_where(row == lane), bc).astype(BF16)
    gc_ref[...] = dot_t(ones_where(row + states == lane), bc).astype(BF16)


def on_device(
    tm,
    chan,
    inner_x,
    gate_z,
    dt_raw,
    grad_out,
    input_b,
    output_c,
    conv_weight,
    conv_bias,
    decay_log,
    skip_gain,
):
    length, width = inner_x.shape
    states = input_b.shape[1]
    per = length // tm
    assert per % 8 == 0 and length // (S_DEV * tm) >= conv_weight.shape[0] - 1
    wide = width + 2 * states
    vmem = pl.BlockSpec(memory_space=pltpu.VMEM)
    rows = pltpu.VMEM((length, width), F32)
    block = (tm, 2 * per, width)
    sems = pltpu.SemaphoreType.DMA
    limit = 60 * 1024 * 1024
    arrays = (
        inner_x,
        gate_z,
        dt_raw,
        grad_out,
        input_b.T,
        output_c.T,
        conv_weight,
        conv_bias,
        decay_log,
        skip_gain,
    )
    scratch = [
        *[pltpu.VMEM(array.shape, array.dtype) for array in arrays],
        pltpu.VMEM((tm, 2 * per, wide), BF16),
        pltpu.VMEM(block, BF16),
        pltpu.VMEM((tm, 16, width), BF16),
        pltpu.VMEM((tm, 2 * per, wide), BF16),
        pltpu.VMEM(block, BF16),
        pltpu.VMEM((16, width), BF16),
        pltpu.VMEM((16, width), BF16),
        pltpu.VMEM((16, width), BF16),
        pltpu.VMEM((tm, 16, width), BF16),
        pltpu.VMEM((8, 128), F32),
        pltpu.VMEM((tm, 8, 128), F32),
        pltpu.VMEM((length, 128), F32),
        pltpu.VMEM((tm, per, 128), F32),
        pltpu.VMEM(block, BF16),
        pltpu.VMEM(block, BF16),
        pltpu.VMEM((length + 8, width), F32),
        *[rows] * 11,
        pltpu.VMEM((length + 16, width), F32),
        pltpu.VMEM((length * states, 256), F32),
        pltpu.VMEM((length * states, width), F32),
        pltpu.VMEM((3, BLK * states, width), BF16),
        sems((10,)),
        sems((2, tm)),
        sems((2, tm)),
        sems((tm + 1,)),
        sems((2, tm)),
        sems((2, tm)),
        sems((2, chan, tm)),
        sems((2, tm)),
        sems((2, tm)),
    ]
    out_a, out_b, out_p = pl.pallas_call(
        functools.partial(kernel, tm, chan),
        out_shape=[
            jax.ShapeDtypeStruct(block, BF16),
            jax.ShapeDtypeStruct(block, BF16),
            jax.ShapeDtypeStruct((chan, tm, per, 128), F32),
        ],
        in_specs=[pl.BlockSpec(memory_space=pl.ANY)] * 10,
        out_specs=[vmem] * 3,
        scratch_shapes=scratch,
        compiler_params=pltpu.CompilerParams(
            collective_id=0, has_side_effects=True, vmem_limit_bytes=limit
        ),
    )(*arrays)
    wide_out = jax.ShapeDtypeStruct((length, width), BF16)
    thin_out = jax.ShapeDtypeStruct((states, length), BF16)
    gx, gdt, gz, gb, gc = pl.pallas_call(
        functools.partial(unpack_kernel, tm, states, conv_weight.shape[0]),
        out_shape=[wide_out, wide_out, wide_out, thin_out, thin_out],
        in_specs=[vmem] * 3,
        out_specs=[vmem] * 5,
        compiler_params=pltpu.CompilerParams(vmem_limit_bytes=limit),
    )(out_a, out_b, out_p)
    return gx, gdt, gz, gb.T, gc.T


def solution(mesh):
    return jax.shard_map(
        functools.partial(on_device, mesh.shape["tm"], mesh.shape["chan"]),
        mesh=mesh,
        in_specs=(
            P("tm", "chan"),
            P("tm", "chan"),
            P("tm", "chan"),
            P("tm", "chan"),
            P("tm", None),
            P("tm", None),
            P(None, "chan"),
            P("chan"),
            P(None, "chan"),
            P("chan"),
        ),
        out_specs=(P("tm", "chan"), P("tm", "chan"), P("tm", "chan"), P("tm", None), P("tm", None)),
        check_vma=False,
    )
```

```python
import functools

import jax
import jax.numpy as jnp
from jax import lax
from jax.experimental import pallas as pl
from jax.experimental.pallas import tpu as pltpu
from jax.sharding import PartitionSpec as P

S_DEV = 2
BLK = 16
F32 = jnp.float32
BF16 = jnp.bfloat16
MESH = pl.DeviceIdType.MESH


def log2(value):
    assert value & (value - 1) == 0
    return value.bit_length() - 1


def dot(left, right):
    return jnp.dot(left, right, preferred_element_type=F32)


def dot_t(left, right):
    return lax.dot_general(left, right, (((1,), (1,)), ((), ())), preferred_element_type=F32)


def iotas(shape):
    return lax.broadcasted_iota(jnp.int32, shape, 0), lax.broadcasted_iota(jnp.int32, shape, 1)


def ones_where(mask):
    return jnp.where(mask, 1.0, 0.0).astype(BF16)


def fields(packed, half, per, frames):
    partner = packed >> log2(2 * per)
    inside = packed & (2 * per - 1)
    rest = inside & (per - 1)
    spatial = rest >> log2(frames)
    frame = rest & (frames - 1)
    valid = (inside >> log2(per)) == half
    return partner, spatial, frame, valid


def row_of(packed, half, tm, per, frames):
    partner, spatial, frame, valid = fields(packed, half, per, frames)
    row = frame * (S_DEV * tm) + partner * S_DEV + spatial
    return jnp.where(valid, row, -1)


def place_of(packed, half, tm, per, frames):
    partner, spatial, frame, valid = fields(packed, half, per, frames)
    place = spatial * (frames * tm) + partner * frames + frame
    return jnp.where(valid, place, -1)


def pack_matrix(of, half, tm, per, frames, length):
    packed, row = iotas((tm * 2 * per, length))
    return ones_where(of(packed, half, tm, per, frames) == row)


def unpack_matrix(of, half, tm, per, frames, length):
    row, packed = iotas((length, tm * 2 * per))
    return ones_where(of(packed, half, tm, per, frames) == row)


def sigmoid(values):
    return 1.0 / (1.0 + jnp.exp(-values))


def silu_grad(values):
    sigm = sigmoid(values)
    return sigm * (1.0 + values * (1.0 - sigm))


def kernel(
    tm,
    chan,
    x_any,
    z_any,
    dt_any,
    g_any,
    b_any,
    c_any,
    w_any,
    bias_any,
    log_any,
    skip_any,
    out_a,
    out_b,
    out_p,
    x_ref,
    z_ref,
    dt_ref,
    g_ref,
    b_ref,
    c_ref,
    w_ref,
    bias_ref,
    log_ref,
    skip_ref,
    send_1,
    send_2,
    send_h,
    recv_1,
    recv_2,
    recv_h,
    end_up,
    end_down,
    ends_in,
    tot,
    tot_in,
    part,
    part_in,
    send_p,
    send_a,
    send_b,
    xpad,
    pre_s,
    conv_s,
    delta_s,
    u_s,
    dy_s,
    dt_s,
    z_s,
    g_s,
    y_s,
    w_s,
    d_s,
    gp_s,
    bc_s,
    fs_s,
    prod,
    sem_in,
    sem_1,
    sem_2,
    sem_h,
    sem_e,
    sem_t,
    sem_p,
    sem_c,
    sem_a,
    sem_b,
):
    me = lax.axis_index("tm")
    ch = lax.axis_index("chan")
    length, width = x_ref.shape
    states = b_ref.shape[0]
    taps = w_ref.shape[0]
    frames = length // (S_DEV * tm)
    per = S_DEV * frames
    wide = width + 2 * states
    base = width // 128 * 128

    def over_tm(body):
        def step(k, carry):
            body(lax.rem(me + k + 1, tm))
            return carry

        lax.fori_loop(0, tm - 1, step, 0)

    def over_chan(body):
        for j in range(1, chan):
            body(lax.rem(ch + j, chan))

    barrier = pltpu.get_barrier_semaphore()

    def greet(d, c):
        pl.semaphore_signal(
            barrier, inc=1, device_id={"tm": d, "chan": c}, device_id_type=MESH
        )

    over_tm(lambda d: greet(d, ch))
    over_chan(lambda c: greet(me, c))
    outside = (
        x_any, z_any, dt_any, g_any, b_any, c_any, w_any, bias_any, log_any, skip_any
    )
    inside = (x_ref, z_ref, dt_ref, g_ref, b_ref, c_ref, w_ref, bias_ref, log_ref, skip_ref)
    loads = [
        pltpu.make_async_copy(source, target, sem_in.at[k])
        for k, (source, target) in enumerate(zip(outside, inside))
    ]
    for load in loads:
        load.start()
    for load in loads:
        load.wait()

    row, lane = iotas((width, wide))
    ex = ones_where(row == lane)
    row, lane = iotas((states, wide))
    eb = ones_where(lane == row + width)
    ec = ones_where(lane == row + width + states)
    x_ext = dot(x_ref[...], ex).astype(BF16)
    first = pack_matrix(row_of, 0, tm, per, frames, length)
    second = pack_matrix(row_of, 1, tm, per, frames, length)
    dt_ext = dot(dt_ref[...], ex).astype(BF16)
    b_rows = dot_t(first, b_ref[...]).astype(BF16)
    c_rows = dot_t(first, c_ref[...]).astype(BF16)
    one = dot(first, x_ext) + dot(second, dt_ext) + dot(b_rows, eb) + dot(c_rows, ec)
    send_1[...] = one.astype(BF16).reshape(tm, 2 * per, wide)
    packed, row = iotas((tm * 16, length))
    slot = packed & 15
    frame = slot - (8 - frames)
    source = frame * (S_DEV * tm) + (packed >> 4) * S_DEV - 1
    good = (frame >= 0) & (slot < 8) & (packed >= 16)
    halo = ones_where(jnp.where(good, source, -1) == row)
    send_h[...] = dot(halo, x_ref[...]).astype(BF16).reshape(tm, 16, width)

    def copy_tm(src, dst, sems, d, origin):
        return pltpu.make_async_remote_copy(
            src_ref=src,
            dst_ref=dst,
            send_sem=sems.at[0, d],
            recv_sem=sems.at[1, origin],
            device_id={"tm": d},
            device_id_type=MESH,
        )

    def copy_1(d, origin):
        return copy_tm(send_1.at[d], recv_1.at[origin], sem_1, d, origin)

    def copy_2(d, origin):
        return copy_tm(send_2.at[d], recv_2.at[origin], sem_2, d, origin)

    def copy_h(d):
        return pltpu.make_async_remote_copy(
            src_ref=send_h.at[d],
            dst_ref=recv_h,
            send_sem=sem_h.at[d],
            recv_sem=sem_h.at[tm],
            device_id={"tm": d},
            device_id_type=MESH,
        )

    def start_halo(d):
        @pl.when(me == tm - 1)
        def _():
            copy_h(d).start()

    pl.semaphore_wait(barrier, tm + chan - 2)
    over_tm(start_halo)
    over_tm(lambda d: copy_1(d, me).start())
    two = dot(first, z_ref[...]) + dot(second, g_ref[...])
    send_2[...] = two.astype(BF16).reshape(tm, 2 * per, width)
    over_tm(lambda d: copy_2(d, me).start())
    recv_1[me] = send_1[me]
    recv_2[me] = send_2[me]

    rate = -jnp.exp(log_ref[...])
    take_0 = unpack_matrix(place_of, 0, tm, per, frames, length)
    take_1 = unpack_matrix(place_of, 1, tm, per, frames, length)
    row, lane = iotas((BLK, BLK * states))
    sel = ones_where((lane >> log2(states)) == row)
    row, lane = iotas((BLK * states, BLK))
    spread = ones_where((row >> log2(states)) == lane)

    @pl.when(me == tm - 1)
    def _():
        recv_h[...] = send_h[me]

    @pl.when(me != tm - 1)
    def _():
        copy_h(me).wait_recv()

    over_tm(lambda d: copy_1(d, d).wait_recv())
    got_1 = recv_1[...].reshape(tm * 2 * per, wide)
    x_full = dot(take_0, got_1)
    dt_vals = dot(take_1, got_1[:, :width])
    xpad[0:8, :] = recv_h[...].astype(F32)[0:8]
    xpad[8:, :] = x_full[:, :width]
    tail = wide - base
    bc_bf = x_full[:, base:].astype(BF16)
    row, lane = iotas((BLK * states, tail))
    keep = ((lane - (width - base)) & (states - 1)) == (row & (states - 1))
    keep = keep & (lane >= width - base)
    row, lane = iotas((tail, 256))
    fan = ones_where(
        (row >= width - base)
        & (((row - (width - base)) >> log2(states)) == (lane >> 7))
    )
    for block in range(length // BLK):
        rows = dot(spread, bc_bf[block * BLK : (block + 1) * BLK])
        rows = jnp.where(keep, rows, 0.0).astype(BF16)
        bc_s[block * BLK * states : (block + 1) * BLK * states, :] = dot(rows, fan)

    dt_s[...] = dt_vals
    deltas = jnp.maximum(dt_vals, 0.0) + jnp.log(1.0 + jnp.exp(-jnp.abs(dt_vals)))
    delta_s[...] = deltas
    pre = bias_ref[...].reshape(1, width) + w_ref[0:1, :] * xpad[8 - taps + 1 : 8 - taps + 1 + length, :]
    for k in range(1, taps):
        pre = pre + w_ref[k : k + 1, :] * xpad[8 - taps + 1 + k : 8 - taps + 1 + k + length, :]
    pre_s[...] = pre
    conv = pre * sigmoid(pre)
    conv_s[...] = conv
    u_s[...] = deltas * conv
    total = jnp.sum(deltas, axis=0, keepdims=True)
    padded = jnp.concatenate([total, jnp.zeros((1, 128 - width % 128), F32)], axis=1)
    lines = [padded[:, k : k + 128] for k in range(0, width, 128)]
    tot[...] = jnp.concatenate(lines + [jnp.zeros((8 - len(lines), 128), F32)], axis=0)

    def copy_tot(d, origin):
        return copy_tm(tot, tot_in.at[origin], sem_t, d, origin)

    over_tm(lambda d: copy_tot(d, me).start())

    over_tm(lambda d: copy_2(d, d).wait_recv())
    got_2 = recv_2[...].reshape(tm * 2 * per, width)
    z_vals = dot(take_0, got_2)
    g_vals = dot(take_1, got_2)
    z_s[...] = z_vals
    g_s[...] = g_vals
    dy_s[...] = (g_vals * (z_vals * sigmoid(z_vals))).astype(BF16).astype(F32)

    def over_lanes(tile):
        return jnp.concatenate([tile] * (width // 128) + [tile[:, : width % 128]], axis=1)

    def b_at(q):
        return over_lanes(bc_s[pl.ds(pl.multiple_of(q * states, states), states), 0:128])

    def c_at(q):
        return over_lanes(bc_s[pl.ds(pl.multiple_of(q * states, states), states), 128:256])

    zero = jnp.zeros((states, width), F32)

    def local(i, carry):
        state, back = carry
        up = pl.multiple_of(i * 8, 8)
        down = pl.multiple_of(length - 8 - i * 8, 8)
        d_up, u_up = delta_s[pl.ds(up, 8), :], u_s[pl.ds(up, 8), :]
        d_dn, y_dn = delta_s[pl.ds(down, 8), :], dy_s[pl.ds(down, 8), :]
        for j in range(8):
            state = jnp.exp(d_up[j : j + 1] * rate) * state + u_up[j : j + 1] * b_at(up + j)
            m = 7 - j
            back = jnp.exp(d_dn[m : m + 1] * rate) * (y_dn[m : m + 1] * c_at(down + m) + back)
        return state, back

    end, back_end = lax.fori_loop(0, length // 8, local, (zero, zero))
    end_up[...] = end.astype(BF16)
    end_down[...] = back_end.astype(BF16)

    def copy_up(d, origin):
        return copy_tm(end_up, ends_in.at[origin], sem_e, d, origin)

    def copy_down(d, origin):
        return copy_tm(end_down, ends_in.at[origin], sem_e, d, origin)

    def send_end(d):
        @pl.when(d > me)
        def _():
            copy_up(d, me).start()

        @pl.when(d < me)
        def _():
            copy_down(d, me).start()

    over_tm(send_end)

    def through(source):
        lines = tot_in[source]
        pieces = [lines[k : k + 1, : min(128, width - 128 * k)] for k in range(-(-width // 128))]
        return jnp.exp(rate * jnp.concatenate(pieces, axis=1))

    over_tm(lambda d: copy_tot(d, d).wait_recv())

    def enter_up(source, state):
        copy_up(source, source).wait_recv()
        return through(source) * state + ends_in[source].astype(F32)

    def enter_down(turn, back):
        source = tm - 1 - turn
        copy_down(source, source).wait_recv()
        return through(source) * back + ends_in[source].astype(F32)

    state_in = lax.fori_loop(0, me, enter_up, zero)
    back_in = lax.fori_loop(0, tm - 1 - me, enter_down, zero)

    row, lane = iotas((BLK * states, 128))
    at_b = lane == (row & (states - 1))
    at_c = lane == (row & (states - 1)) + states
    ones = jnp.ones((width, 128), BF16)
    skip = skip_ref[...].reshape(1, width)

    def picked(product, where):
        sums = jnp.where(where, dot(product, ones), 0.0)
        high = sums.astype(BF16)
        low = (sums - high.astype(F32)).astype(BF16)
        return dot(sel, high) + dot(sel, low)

    def forward(i, state):
        start = pl.multiple_of(i * BLK, BLK)
        here = pl.ds(start, BLK)
        d_blk, u_blk, y_blk = delta_s[here, :], u_s[here, :], dy_s[here, :]
        for j in range(BLK):
            kept = jnp.exp(d_blk[j : j + 1] * rate) * state
            state = kept + u_blk[j : j + 1] * b_at(start + j)
            fs_s[pl.ds(pl.multiple_of((start + j) * states, states), states), :] = kept
            prod[0, j * states : (j + 1) * states, :] = (c_at(start + j) * state).astype(BF16)
            prod[1, j * states : (j + 1) * states, :] = (y_blk[j : j + 1] * state).astype(BF16)
        y_s[here, :] = dot(sel, prod[0]) + skip * conv_s[here, :]
        part[here, :] = picked(prod[1], at_c)
        return state

    lax.fori_loop(0, length // BLK, forward, state_in)

    def backward(turn, back):
        start = pl.multiple_of(length - BLK - turn * BLK, BLK)
        here = pl.ds(start, BLK)
        d_blk, u_blk, y_blk = delta_s[here, :], u_s[here, :], dy_s[here, :]
        for j in reversed(range(BLK)):
            adjoint = y_blk[j : j + 1] * c_at(start + j) + back
            back = jnp.exp(d_blk[j : j + 1] * rate) * adjoint
            kept = fs_s[pl.ds(pl.multiple_of((start + j) * states, states), states), :]
            rows = slice(j * states, (j + 1) * states)
            prod[0, rows, :] = (adjoint * b_at(start + j)).astype(BF16)
            prod[1, rows, :] = (adjoint * u_blk[j : j + 1]).astype(BF16)
            prod[2, rows, :] = (adjoint * rate * kept).astype(BF16)
        w_s[here, :] = dot(sel, prod[0])
        d_s[here, :] = dot(sel, prod[2])
        part[here, :] = part[here, :] + picked(prod[1], at_b)
        return back

    lax.fori_loop(0, length // BLK, backward, back_in)

    def copy_a(d, origin):
        return copy_tm(send_a.at[d], out_a.at[origin], sem_a, d, origin)

    def copy_b(d, origin):
        return copy_tm(send_b.at[d], out_b.at[origin], sem_b, d, origin)

    def copy_p(d, origin):
        return copy_tm(send_p.at[d], out_p.at[0, origin], sem_p, d, origin)

    def copy_part(c, origin):
        return pltpu.make_async_remote_copy(
            src_ref=part,
            dst_ref=part_in.at[origin],
            send_sem=sem_c.at[0, c],
            recv_sem=sem_c.at[1, origin],
            device_id={"chan": c},
            device_id_type=MESH,
        )

    over_chan(lambda c: copy_part(c, ch).start())

    deltas = delta_s[...]
    weighted = w_s[...]
    grad_pre = (skip * dy_s[...] + deltas * weighted) * silu_grad(pre_s[...])
    gp_s[0:8, :] = jnp.zeros((8, width), F32)
    gp_s[8 : 8 + length, :] = grad_pre
    gp_s[8 + length :, :] = jnp.zeros((8, width), F32)
    grad_x = w_ref[0:1, :] * gp_s[taps - 1 : taps + 7 + length, :]
    for k in range(1, taps):
        grad_x = grad_x + w_ref[k : k + 1, :] * gp_s[taps - 1 - k : taps + 7 - k + length, :]
    packed, row = iotas((tm * 2 * per, length + 8))
    place = place_of(packed, 0, tm, per, frames)
    slot = packed & (2 * per - 1)
    spill = (packed >= (tm - 1) * 2 * per) & (slot > 2 * per - taps)
    column = jnp.where(place >= 0, place + 8, jnp.where(spill, slot + 8 - 2 * per, -1))
    both = dot(ones_where(column == row), grad_x.astype(BF16)).astype(BF16)
    send_b[...] = both.reshape(tm, 2 * per, width)
    over_tm(lambda d: copy_b(d, me).start())

    give_0 = pack_matrix(place_of, 0, tm, per, frames, length)
    give_1 = pack_matrix(place_of, 1, tm, per, frames, length)
    grad_dt = ((d_s[...] + conv_s[...] * weighted) * sigmoid(dt_s[...])).astype(BF16)
    seq_y = y_s[...].astype(BF16).astype(F32)
    grad_z = (g_s[...] * seq_y * silu_grad(z_s[...])).astype(BF16)
    both = (dot(give_0, grad_dt) + dot(give_1, grad_z)).astype(BF16)
    send_a[...] = both.reshape(tm, 2 * per, width)
    over_tm(lambda d: copy_a(d, me).start())
    packed, row = iotas((tm * per, length))
    place = ((packed & (per - 1)) >> log2(frames)) * (frames * tm)
    place = place + (packed >> log2(per)) * frames + (packed & (frames - 1))
    give = ones_where(place == row)
    over_chan(lambda c: copy_part(c, c).wait_recv())
    part_in[ch] = part[...]
    sums = part_in[0]
    for k in range(1, chan):
        sums = sums + part_in[k]
    high = sums.astype(BF16)
    low = (sums - high.astype(F32)).astype(BF16)
    send_p[...] = (dot(give, high) + dot(give, low)).reshape(tm, per, 128)
    over_tm(lambda d: copy_p(d, me).start())
    out_p[0, me] = send_p[me]
    out_b[me] = send_b[me]
    out_a[me] = send_a[me]

    over_tm(lambda d: copy_1(d, me).wait_send())
    over_tm(lambda d: copy_2(d, me).wait_send())

    def end_halo(d):
        @pl.when(me == tm - 1)
        def _():
            copy_h(d).wait_send()

    over_tm(end_halo)

    def end_ends(d):
        @pl.when(d > me)
        def _():
            copy_up(d, me).wait_send()

        @pl.when(d < me)
        def _():
            copy_down(d, me).wait_send()

    over_tm(end_ends)
    over_tm(lambda d: copy_tot(d, me).wait_send())
    over_tm(lambda d: copy_p(d, me).wait_send())
    over_chan(lambda c: copy_part(c, ch).wait_send())
    over_tm(lambda d: copy_a(d, me).wait_send())
    over_tm(lambda d: copy_b(d, me).wait_send())
    over_tm(lambda d: copy_a(d, d).wait_recv())
    over_tm(lambda d: copy_b(d, d).wait_recv())
    over_tm(lambda d: copy_p(d, d).wait_recv())


def unpack_kernel(tm, states, taps, a_ref, b_ref, p_ref, gx_ref, gdt_ref, gz_ref, gb_ref, gc_ref):
    length, width = gx_ref.shape
    frames = length // (S_DEV * tm)
    per = S_DEV * frames
    take_0 = unpack_matrix(row_of, 0, tm, per, frames, length)
    take_1 = unpack_matrix(row_of, 1, tm, per, frames, length)
    row, packed = iotas((length, tm * 2 * per))
    slot = packed & (2 * per - 1)
    owner = (packed >> log2(2 * per)) - 1
    frame = slot - 2 * per + frames
    added = frame * (S_DEV * tm) + owner * S_DEV + S_DEV - 1
    added = jnp.where((slot > 2 * per - taps) & (owner >= 0), added, -1)
    both = ones_where((row_of(packed, 0, tm, per, frames) == row) | (added == row))
    got_a = a_ref[...].reshape(tm * 2 * per, width)
    got_b = b_ref[...].reshape(tm * 2 * per, width)
    gdt_ref[...] = dot(take_0, got_a).astype(BF16)
    gz_ref[...] = dot(take_1, got_a).astype(BF16)
    gx_ref[...] = dot(both, got_b).astype(BF16)
    sums = p_ref[0]
    for k in range(1, p_ref.shape[0]):
        sums = sums + p_ref[k]
    row, packed = iotas((length, tm * per))
    source = (packed & (frames - 1)) * (S_DEV * tm) + (packed >> log2(per)) * S_DEV
    source = source + ((packed & (per - 1)) >> log2(frames))
    thin = sums.reshape(tm * per, 128).astype(BF16)
    bc = dot(ones_where(source == row), thin).astype(BF16)
    row, lane = iotas((states, 128))
    gb_ref[...] = dot_t(ones_where(row == lane), bc).astype(BF16)
    gc_ref[...] = dot_t(ones_where(row + states == lane), bc).astype(BF16)


def on_device(
    tm,
    chan,
    inner_x,
    gate_z,
    dt_raw,
    grad_out,
    input_b,
    output_c,
    conv_weight,
    conv_bias,
    decay_log,
    skip_gain,
):
    length, width = inner_x.shape
    states = input_b.shape[1]
    per = length // tm
    assert per % 8 == 0 and length // (S_DEV * tm) >= conv_weight.shape[0] - 1
    wide = width + 2 * states
    vmem = pl.BlockSpec(memory_space=pltpu.VMEM)
    rows = pltpu.VMEM((length, width), F32)
    block = (tm, 2 * per, width)
    sems = pltpu.SemaphoreType.DMA
    limit = 60 * 1024 * 1024
    arrays = (
        inner_x,
        gate_z,
        dt_raw,
        grad_out,
        input_b.T,
        output_c.T,
        conv_weight,
        conv_bias,
        decay_log,
        skip_gain,
    )
    scratch = [
        *[pltpu.VMEM(array.shape, array.dtype) for array in arrays],
        pltpu.VMEM((tm, 2 * per, wide), BF16),
        pltpu.VMEM(block, BF16),
        pltpu.VMEM((tm, 16, width), BF16),
        pltpu.VMEM((tm, 2 * per, wide), BF16),
        pltpu.VMEM(block, BF16),
        pltpu.VMEM((16, width), BF16),
        pltpu.VMEM((16, width), BF16),
        pltpu.VMEM((16, width), BF16),
        pltpu.VMEM((tm, 16, width), BF16),
        pltpu.VMEM((8, 128), F32),
        pltpu.VMEM((tm, 8, 128), F32),
        pltpu.VMEM((length, 128), F32),
        pltpu.VMEM((chan, length, 128), F32),
        pltpu.VMEM((tm, per, 128), F32),
        pltpu.VMEM(block, BF16),
        pltpu.VMEM(block, BF16),
        pltpu.VMEM((length + 8, width), F32),
        *[rows] * 11,
        pltpu.VMEM((length + 16, width), F32),
        pltpu.VMEM((length * states, 256), F32),
        pltpu.VMEM((length * states, width), F32),
        pltpu.VMEM((3, BLK * states, width), BF16),
        sems((10,)),
        sems((2, tm)),
        sems((2, tm)),
        sems((tm + 1,)),
        sems((2, tm)),
        sems((2, tm)),
        sems((2, tm)),
        sems((2, chan)),
        sems((2, tm)),
        sems((2, tm)),
    ]
    out_a, out_b, out_p = pl.pallas_call(
        functools.partial(kernel, tm, chan),
        out_shape=[
            jax.ShapeDtypeStruct(block, BF16),
            jax.ShapeDtypeStruct(block, BF16),
            jax.ShapeDtypeStruct((1, tm, per, 128), F32),
        ],
        in_specs=[pl.BlockSpec(memory_space=pl.ANY)] * 10,
        out_specs=[vmem] * 3,
        scratch_shapes=scratch,
        compiler_params=pltpu.CompilerParams(
            collective_id=0, has_side_effects=True, vmem_limit_bytes=limit
        ),
    )(*arrays)
    wide_out = jax.ShapeDtypeStruct((length, width), BF16)
    thin_out = jax.ShapeDtypeStruct((states, length), BF16)
    gx, gdt, gz, gb, gc = pl.pallas_call(
        functools.partial(unpack_kernel, tm, states, conv_weight.shape[0]),
        out_shape=[wide_out, wide_out, wide_out, thin_out, thin_out],
        in_specs=[vmem] * 3,
        out_specs=[vmem] * 5,
        compiler_params=pltpu.CompilerParams(vmem_limit_bytes=limit),
    )(out_a, out_b, out_p)
    return gx, gdt, gz, gb.T, gc.T


def solution(mesh):
    return jax.shard_map(
        functools.partial(on_device, mesh.shape["tm"], mesh.shape["chan"]),
        mesh=mesh,
        in_specs=(
            P("tm", "chan"),
            P("tm", "chan"),
            P("tm", "chan"),
            P("tm", "chan"),
            P("tm", None),
            P("tm", None),
            P(None, "chan"),
            P("chan"),
            P(None, "chan"),
            P("chan"),
        ),
        out_specs=(P("tm", "chan"), P("tm", "chan"), P("tm", "chan"), P("tm", None), P("tm", None)),
        check_vma=False,
    )
```
